32 devices in a mesh: member: 2 (over x), lat: 8 (over z, y), lon: 2 (over core).
Axes of the slice: x: 2, y: 2, z: 4, core: 2. Of those that a mesh axis runs over, the one named last changes fastest.
Arguments:
- activations: bfloat16 [512, 16, 1440], P('member', 'lat', 'lon'), parts along dimension 0, may hold values from -6 to 6
- cotangent: bfloat16 [512, 16, 1440], P('member', 'lat', 'lon'), parts along dimension 0, may hold values from -6 to 6
- mixing: bfloat16 [9, 256, 256], replicated, may hold values from -0.125 to 0.125
- psi_value: bfloat16 [16, 3, 33], replicated, may hold values from -3 to 3
- basis_index: int32 [16, 3, 33], replicated, may hold values from 0 to 8
- band_width: int32 [16, 3], replicated, may hold values from 1 to 16, as said below
Outputs:
- block_out: bfloat16 [512, 16, 1440], P('member', 'lat', 'lon'), parts along dimension 0
- grad_input: bfloat16 [512, 16, 1440], P('member', 'lat', 'lon'), parts along dimension 0
- grad_mixing: float32 [18, 256, 256], P('member'), parts along dimension 0
The draws below stay inside these ranges and needn't reach their ends.
There are 2 independent parts, one for each index of `member`. The reference program is written for one: setup_inputs(seed, part) draws one part's arguments, and reference() takes and returns one part's arrays. A program takes and returns all parts, laid end to end along the dimension named above; an argument that names none is the same for every part. Nothing has to cross between parts.
Inputs may be any that keep to these rules, and one draw needn't show every extreme that they name: `band_width`: widest at the two poles, where it is 16, and narrow near the equator.
All inputs are finite; a program needn't handle non-finite values.
Results may differ from the reference program's by a relative error of at most 0.0057.
Values may be sent and summed in bfloat16 or wider, within the bound.
No kernel may reach another device: no remote copies, remote signals or barrier semaphores. Data moves between devices by JAX's collectives and lax.ppermute only.
A program may use at most 128 MiB of HBM per device.

```python
import math
import jax
import jax.numpy as jnp
from jax import lax

CHANNELS = 256
KERNELS = 9
HALF = 16
NLON = 1440
TAPS = 33
NLAT = 16


def draw_band_width(key, part):
    key = jax.random.fold_in(key, 3)
    latitudes = jnp.arange(NLAT, dtype=jnp.int32)
    polar = jnp.minimum(latitudes, NLAT - 1 - latitudes)
    spread = 3 * HALF // (2 * polar + 3)
    jitter = jax.random.randint(key, (NLAT, 3), 0, 3, dtype=jnp.int32)
    return jnp.minimum(HALF, 1 + spread[:, None] + jitter).astype(jnp.int32)


def with_ends(entries, key, low, largest):
    place = [jax.random.randint(jax.random.fold_in(key, axis), (), 0, length) for axis, length in enumerate(entries.shape)]
    widest = entries.shape.index(max(entries.shape))
    beside = place[:widest] + [(place[widest] + 1) % entries.shape[widest]] + place[widest + 1:]
    return entries.at[tuple(place)].set(low).at[tuple(beside)].set(largest)


def block_levels(stream_key, extent, split, least, top_value):
    loudness, own = 1.0, jax.random.fold_in(stream_key, 6)
    for dim, shards_of in split:
        steps = jnp.exp(jax.random.uniform(jax.random.fold_in(own, dim), (shards_of,), jnp.float32, least / len(split), top_value / len(split)))
        loudness = loudness * jnp.repeat(steps, extent[dim] // shards_of).reshape([-1 if axis == dim else 1 for axis in range(len(extent))])
    return loudness


def gaussian(stream_key, extent, scale, most, cuts=(), kind=jnp.bfloat16):
    drawn = scale * jax.random.normal(stream_key, extent, jnp.float32)
    if cuts:
        drawn = drawn * block_levels(stream_key, extent, cuts, -0.22, 0.18)
    return jnp.clip(drawn, -most, most).astype(kind)


def setup_inputs(seed: int = 0, part: int = 0) -> dict:
    arg_keys = jax.random.split(jax.random.key(seed), 7)
    part_splits = jax.random.split(jax.random.fold_in(arg_keys[6], part), 7)
    activations = gaussian(part_splits[0], (CHANNELS, NLAT, NLON), 1.0, 6.0, ((1, 8), (2, 2)))
    cotangent = gaussian(part_splits[1], (CHANNELS, NLAT, NLON), 1.0, 6.0, ((1, 8), (2, 2)))
    mixing = gaussian(arg_keys[2], (KERNELS, CHANNELS, CHANNELS), (KERNELS * CHANNELS) ** -0.5, 0.125)
    psi_value = gaussian(arg_keys[3], (NLAT, 3, TAPS), 0.5, 3.0)
    basis_index = with_ends(jax.random.randint(arg_keys[4], (NLAT, 3, TAPS), 0, KERNELS), jax.random.fold_in(arg_keys[4], 1), 0, KERNELS - 1).astype(jnp.int32)
    band_width = draw_band_width(jax.random.fold_in(arg_keys[6], 71), part)
    return dict(activations=activations, cotangent=cotangent, mixing=mixing, psi_value=psi_value, basis_index=basis_index, band_width=band_width)


def gelu_value(hidden):
    return 0.5 * hidden * (1.0 + jax.scipy.special.erf(hidden / math.sqrt(2.0)))

def gelu_slope(hidden):
    return 0.5 * (1.0 + jax.scipy.special.erf(hidden / math.sqrt(2.0))) + hidden * jnp.exp(-0.5 * hidden * hidden) / math.sqrt(2.0 * math.pi)

def coefficients(psi_value, basis_index, band_width):
    offsets = jnp.arange(TAPS, dtype=jnp.int32) - HALF
    inband = jnp.abs(offsets)[None, None, :] <= band_width[:, :, None]
    kinds = jnp.arange(KERNELS, dtype=jnp.int32)
    picked = (basis_index[:, None] == kinds[None, :, None, None]) & inband[:, None]
    return jnp.where(picked, psi_value.astype(jnp.float32)[:, None], jnp.float32(0.0))

def reference(activations, cotangent, mixing, psi_value, basis_index, band_width):
    kernel_taps = coefficients(psi_value, basis_index, band_width)
    field = jnp.moveaxis(activations, 1, 0).astype(jnp.float32)
    padded = jnp.pad(field, ((1, 1), (0, 0), (0, 0)))
    upstream = jnp.moveaxis(cotangent, 1, 0).astype(jnp.float32)
    weights = mixing.astype(jnp.float32)

    def visit(carry, row):
        grad_w, grad_x = carry
        rows_near = lax.dynamic_slice_in_dim(padded, row, 3, 0)
        unfolded = jnp.stack([jnp.roll(rows_near, -(tap - HALF), axis=-1) for tap in range(TAPS)])
        row_taps = lax.dynamic_index_in_dim(kernel_taps, row, 0, keepdims=False)
        basis_out = jnp.einsum('krt,trcj->kcj', row_taps, unfolded).astype(jnp.bfloat16)
        basis_f = lax.optimization_barrier(basis_out).astype(jnp.float32)
        hidden = jnp.einsum('koc,kcj->oj', weights, basis_f)
        own_row = lax.dynamic_index_in_dim(field, row, 0, keepdims=False)
        out_row = (own_row + gelu_value(hidden)).astype(jnp.bfloat16)
        grad_row = lax.dynamic_index_in_dim(upstream, row, 0, keepdims=False)
        slope = (grad_row * gelu_slope(hidden)).astype(jnp.bfloat16)
        slope_f = lax.optimization_barrier(slope).astype(jnp.float32)
        grad_w = grad_w + jnp.einsum('oj,kcj->koc', slope_f, basis_f)
        basis_grad = jnp.einsum('koc,oj->kcj', weights, slope_f).astype(jnp.bfloat16)
        bgrad_f = lax.optimization_barrier(basis_grad).astype(jnp.float32)
        spread = jnp.einsum('krt,kcj->trcj', row_taps, bgrad_f)
        back = jnp.roll(spread[0], -HALF, axis=-1)
        for tap in range(1, TAPS):
            back = back + jnp.roll(spread[tap], tap - HALF, axis=-1)
        current = lax.dynamic_slice_in_dim(grad_x, row, 3, 0)
        grad_x = lax.dynamic_update_slice_in_dim(grad_x, current + back, row, 0)
        return ((grad_w, grad_x), out_row)
    start = (jnp.zeros((KERNELS, CHANNELS, CHANNELS), jnp.float32), jnp.zeros((NLAT + 2, CHANNELS, NLON), jnp.float32))
    (grad_w, grad_x), out_rows = lax.scan(visit, start, jnp.arange(NLAT, dtype=jnp.int32))
    block_out = jnp.moveaxis(out_rows, 0, 1)
    grad_input = jnp.moveaxis((upstream + grad_x[1:-1]).astype(jnp.bfloat16), 0, 1)
    return (block_out, grad_input, grad_w / NLAT)
```

```python
import math

import jax
import jax.numpy as jnp
from jax import lax
from jax.sharding import PartitionSpec as P

KERNELS = 9
HALF = 16
TAPS = 2 * HALF + 1
BLK = 120
WIN = BLK + 2 * HALF


def lat_halo(rows):
    count = lax.axis_size("lat")
    forward = [(i, i + 1) for i in range(count - 1)]
    backward = [(target, source) for source, target in forward]
    above = lax.ppermute(rows[-1:], "lat", forward)
    below = lax.ppermute(rows[:1], "lat", backward)
    return jnp.concatenate([above, rows, below], axis=0)


def lon_halo(rows):
    count = lax.axis_size("lon")
    west, east = rows[:, :HALF], rows[:, -HALF:]
    if count == 2:
        both = lax.ppermute(jnp.concatenate([east, west], axis=1), "lon", [(0, 1), (1, 0)])
        low, high = both[:, :HALF], both[:, HALF:]
    else:
        forward = [(i, (i + 1) % count) for i in range(count)]
        low = lax.ppermute(east, "lon", forward)
        high = lax.ppermute(west, "lon", [(target, source) for source, target in forward])
    return jnp.concatenate([low, rows, high], axis=1)


def gelu_parts(hidden):
    cdf = 0.5 * (1.0 + lax.erf(hidden * (1.0 / math.sqrt(2.0))))
    slope = cdf + hidden * jnp.exp(-0.5 * hidden * hidden) * (1.0 / math.sqrt(2.0 * math.pi))
    return hidden * cdf, slope


def coefficients(psi_value, basis_index, band_width):
    offsets = jnp.arange(TAPS, dtype=jnp.int32) - HALF
    inband = jnp.abs(offsets)[None, None, :] <= band_width[:, :, None]
    kinds = jnp.arange(KERNELS, dtype=jnp.int32)
    picked = (basis_index[:, None] == kinds[None, :, None, None]) & inband[:, None]
    return jnp.where(picked, psi_value[:, None], jnp.zeros((), jnp.bfloat16))


def local_taps(psi_value, basis_index, band_width, first_row, rows):
    value_pad = jnp.pad(psi_value, ((1, 1), (0, 0), (0, 0)))
    basis_pad = jnp.pad(basis_index, ((1, 1), (0, 0), (0, 0)))
    width_pad = jnp.pad(band_width, ((1, 1), (0, 0)))
    near = coefficients(
        lax.dynamic_slice_in_dim(value_pad, first_row, rows + 2, 0),
        lax.dynamic_slice_in_dim(basis_pad, first_row, rows + 2, 0),
        lax.dynamic_slice_in_dim(width_pad, first_row, rows + 2, 0),
    )
    direct = near[1 : rows + 1]
    adjoint = jnp.stack(
        [near[offset : offset + rows, :, 2 - offset, ::-1] for offset in range(3)], axis=2
    )
    return direct, adjoint


def banded_tables(taps):
    tap = jnp.arange(WIN, dtype=jnp.int32)[None, :] - jnp.arange(BLK, dtype=jnp.int32)[:, None]
    tap_ids = jnp.arange(TAPS, dtype=jnp.int32)[:, None, None]
    selector = (tap_ids == tap[None]).astype(jnp.bfloat16)
    tables = jnp.einsum("nkrt,tjw->nkjrw", taps, selector, preferred_element_type=jnp.float32)
    return tables.astype(jnp.bfloat16)


def banded(tables, wide, rows, columns):
    blocks = columns // BLK
    windows = jnp.stack([wide[:, b * BLK : b * BLK + WIN] for b in range(blocks)], axis=1)
    stacked = jnp.stack([windows[offset : offset + rows] for offset in range(3)], axis=2)
    out = jnp.einsum("nkjrw,nbrwc->nbjkc", tables, stacked, preferred_element_type=jnp.float32)
    return out.astype(jnp.bfloat16).reshape(rows * columns, -1)


def halves(part, bit):
    size = part.shape[0] // 2
    keep = lax.dynamic_slice_in_dim(part, bit * size, size, 0)
    give = lax.dynamic_slice_in_dim(part, (1 - bit) * size, size, 0)
    return keep, give


def joined(own, other, bit):
    return jnp.where(
        bit == 0, jnp.concatenate([own, other], 0), jnp.concatenate([other, own], 0)
    )


def summed(part):
    stages = []
    for axis in ("lon", "lat"):
        count = lax.axis_size(axis)
        step = 1
        while step < count:
            pairs = [(i, i ^ step) for i in range(count)]
            stages.append((axis, pairs, (lax.axis_index(axis) // step) % 2))
            step *= 2
    for axis, pairs, bit in stages:
        keep, give = halves(part, bit)
        got = lax.ppermute(give.astype(jnp.bfloat16), axis, pairs)
        part = keep + got.astype(jnp.float32)
    part = part.astype(jnp.bfloat16)
    for axis, pairs, bit in reversed(stages):
        part = joined(part, lax.ppermute(part, axis, pairs), bit)
    return part.astype(jnp.float32)


def on_device(activations, cotangent, mixing, psi_value, basis_index, band_width):
    channels, rows, columns = activations.shape
    total_rows = lax.axis_size("lat") * rows
    first_row = lax.axis_index("lat") * rows
    direct, adjoint = local_taps(psi_value, basis_index, band_width, first_row, rows)
    direct_tables, adjoint_tables = banded_tables(direct), banded_tables(adjoint)
    field = activations.transpose(1, 2, 0)
    upstream = cotangent.transpose(1, 2, 0).reshape(rows * columns, channels)
    to_hidden = mixing.transpose(0, 2, 1).reshape(KERNELS * channels, channels)
    to_input = mixing.reshape(KERNELS * channels, channels)

    basis_out = banded(direct_tables, lat_halo(lon_halo(field)), rows, columns)
    hidden = jnp.dot(basis_out, to_hidden, preferred_element_type=jnp.float32)
    value, derivative = gelu_parts(hidden)
    upstream_f = upstream.astype(jnp.float32)
    block_out = (field.reshape(rows * columns, channels).astype(jnp.float32) + value).astype(
        jnp.bfloat16
    )
    slope = (upstream_f * derivative).astype(jnp.bfloat16)
    partial = jnp.einsum(
        "po,pkc->koc",
        slope,
        basis_out.reshape(rows * columns, KERNELS, channels),
        preferred_element_type=jnp.float32,
    ) * (1.0 / total_rows)
    grad_mixing = summed(partial.reshape(KERNELS * channels, channels)).reshape(mixing.shape)
    slope_wide = lat_halo(lon_halo(slope.reshape(rows, columns, channels)))
    spread = banded(adjoint_tables, slope_wide, rows, columns)
    backward = jnp.dot(spread, to_input, preferred_element_type=jnp.float32)
    grad_input = (upstream_f + backward).astype(jnp.bfloat16)

    def home(block):
        return block.reshape(rows, columns, channels).transpose(2, 0, 1)

    return home(block_out), home(grad_input), grad_mixing


def solution(mesh):
    in_specs = (P("member", "lat", "lon"), P("member", "lat", "lon"), P(), P(), P(), P())
    out_specs = (P("member", "lat", "lon"), P("member", "lat", "lon"), P("member", None, None))
    return jax.shard_map(
        on_device, mesh=mesh, in_specs=in_specs, out_specs=out_specs, check_vma=False
    )
```

```python
import math

import jax
import jax.numpy as jnp
from jax import lax
from jax.experimental import pallas as pl
from jax.experimental.pallas import tpu as pltpu
from jax.sharding import PartitionSpec as P

KERNELS = 9
HALF = 16
TAPS = 2 * HALF + 1
BLK = 128
WIN = BLK + 2 * HALF
DEPTH = 512
VMEM = pl.BlockSpec(memory_space=pltpu.VMEM)
BF16, F32 = jnp.bfloat16, jnp.float32


def call(kernel, out_shape, scratch, flops, size, *operands, name):
    return pl.pallas_call(
        kernel,
        out_shape=out_shape,
        in_specs=[VMEM] * len(operands),
        out_specs=jax.tree.map(lambda _: VMEM, out_shape),
        scratch_shapes=scratch,
        compiler_params=pltpu.CompilerParams(vmem_limit_bytes=48 * 2**20),
        cost_estimate=pl.CostEstimate(flops=flops, bytes_accessed=size, transcendentals=0),
        name=name,
    )(*operands)


def tables_kernel(lines_ref, out_ref):
    rows = lines_ref.shape[0]
    for row in range(rows):
        for kind in range(KERNELS):
            line = jnp.broadcast_to(lines_ref[row, kind : kind + 1, :], (BLK, DEPTH))
            out_ref[row, kind * BLK : (kind + 1) * BLK, :] = pltpu.roll(
                line, 0, 1, stride=1, stride_axis=0
            ).astype(BF16)


def banded_tables(taps):
    lead = taps.shape[0]
    lines = jnp.pad(taps.astype(F32), ((0, 0), (0, 0), (0, 0), (0, WIN - TAPS)))
    lines = jnp.pad(lines.reshape(lead, KERNELS, 3 * WIN), ((0, 0), (0, 0), (0, DEPTH - 3 * WIN)))
    shape = jax.ShapeDtypeStruct((lead, KERNELS * BLK, DEPTH), BF16)
    return call(tables_kernel, shape, [], 0, 6_000_000, lines, name="tables")


def starts_of(columns):
    return [min(b * BLK, columns - BLK) for b in range(-(-columns // BLK))]


def spread_rows(table_ref, wide_ref, buffer_ref, own_ref, lon_ref, above_ref, below_ref):
    rows, columns, channels = own_ref.shape
    wide_ref[0] = above_ref[0]
    wide_ref[rows + 1] = below_ref[0]
    for row in range(rows):
        wide_ref[row + 1, 0:HALF] = lon_ref[row, 0:HALF]
        wide_ref[row + 1, HALF : HALF + columns] = own_ref[row]
        wide_ref[row + 1, HALF + columns :] = lon_ref[row, HALF:]
    for row in range(rows):
        for start in starts_of(columns):
            window = jnp.concatenate(
                [wide_ref[row + offset, start : start + WIN] for offset in range(3)], axis=0
            )
            base = row * columns + start
            for kind in range(KERNELS):
                out = jnp.dot(
                    table_ref[row, kind * BLK : (kind + 1) * BLK, : 3 * WIN],
                    window,
                    preferred_element_type=F32,
                )
                buffer_ref[base : base + BLK, kind * channels : (kind + 1) * channels] = (
                    out.astype(BF16)
                )


def gelu_parts(hidden):
    cdf = 0.5 * (1.0 + lax.erf(hidden * (1.0 / math.sqrt(2.0))))
    slope = cdf + hidden * jnp.exp(-0.5 * hidden * hidden) * (1.0 / math.sqrt(2.0 * math.pi))
    return hidden * cdf, slope


def forward_kernel(
    scale, own_ref, lon_ref, above_ref, below_ref, table_ref, mix_ref, cot_ref,
    out_ref, slope_ref, keep_ref, give_ref, wide_ref, buffer_ref, turned_ref,
):
    rows, columns, channels = own_ref.shape
    spread_rows(table_ref, wide_ref, buffer_ref, own_ref, lon_ref, above_ref, below_ref)
    step = 240
    for row in range(rows):
        for start in range(0, columns, step):
            at = row * columns + start
            hidden = jnp.dot(
                buffer_ref[at : at + step, :], mix_ref[...], preferred_element_type=F32
            )
            value, derivative = gelu_parts(hidden)
            part = slice(start, start + step)
            out_ref[row, part] = (own_ref[row, part].astype(F32) + value).astype(BF16)
            slope = (cot_ref[row, part].astype(F32) * derivative).astype(BF16)
            slope_ref[row, part] = slope
        turned_ref[:, row * columns : (row + 1) * columns] = slope_ref[row].T
    first = lax.axis_index("lon") == 0
    half = channels // 2
    for kind in range(KERNELS):
        grad = scale * jnp.dot(
            turned_ref[...],
            buffer_ref[:, kind * channels : (kind + 1) * channels],
            preferred_element_type=F32,
        )
        low, high = grad[:half], grad[half:]
        keep_ref[kind] = jnp.where(first, low, high)
        give_ref[kind] = jnp.where(first, high, low).astype(BF16)


def backward_kernel(
    own_ref, lon_ref, above_ref, below_ref, table_ref, mix_ref, cot_ref,
    out_ref, wide_ref, buffer_ref,
):
    rows, columns, channels = own_ref.shape
    spread_rows(table_ref, wide_ref, buffer_ref, own_ref, lon_ref, above_ref, below_ref)
    step = 240
    for row in range(rows):
        for start in range(0, columns, step):
            at = row * columns + start
            grad = jnp.dot(
                buffer_ref[at : at + step, :], mix_ref[...], preferred_element_type=F32
            )
            part = slice(start, start + step)
            out_ref[row, part] = (cot_ref[row, part].astype(F32) + grad).astype(BF16)


def scratch_of(field):
    rows, columns, channels = field.shape
    return [
        pltpu.VMEM((rows + 2, columns + 2 * HALF, channels), BF16),
        pltpu.VMEM((rows * columns, KERNELS * channels), BF16),
    ]


def forward(field, lon, above, below, table, mix, upstream, scale):
    rows, columns, channels = field.shape
    halved = (KERNELS, channels // 2, channels)
    shapes = (
        jax.ShapeDtypeStruct(field.shape, BF16),
        jax.ShapeDtypeStruct(field.shape, BF16),
        jax.ShapeDtypeStruct(halved, F32),
        jax.ShapeDtypeStruct(halved, BF16),
    )
    turned = pltpu.VMEM((channels, rows * columns), BF16)

    def kernel(*refs):
        forward_kernel(scale, *refs)

    return call(
        kernel, shapes, scratch_of(field) + [turned], 7 * 10**9, 8 * 10**6,
        field, lon, above, below, table, mix, upstream, name="forward",
    )


def backward(slope, lon, above, below, table, mix, upstream):
    return call(
        backward_kernel, jax.ShapeDtypeStruct(slope.shape, BF16), scratch_of(slope),
        5 * 10**9, 8 * 10**6, slope, lon, above, below, table, mix, upstream, name="backward",
    )


def lat_halo(rows):
    count = lax.axis_size("lat")
    forward = [(i, i + 1) for i in range(count - 1)]
    backward = [(target, source) for source, target in forward]
    above = lax.ppermute(rows[-1:], "lat", forward)
    below = lax.ppermute(rows[:1], "lat", backward)
    return above, below


def lon_halo(rows):
    count = lax.axis_size("lon")
    west, east = rows[:, :HALF], rows[:, -HALF:]
    if count == 2:
        return lax.ppermute(jnp.concatenate([east, west], axis=1), "lon", [(0, 1), (1, 0)])
    forward = [(i, (i + 1) % count) for i in range(count)]
    low = lax.ppermute(east, "lon", forward)
    high = lax.ppermute(west, "lon", [(target, source) for source, target in forward])
    return jnp.concatenate([low, high], axis=1)


def halos(rows):
    lon = lon_halo(rows)
    wide = jnp.concatenate([lon[:, :HALF], rows, lon[:, HALF:]], axis=1)
    above, below = lat_halo(wide)
    return lon, above, below


def coefficients(psi_value, basis_index, band_width):
    offsets = jnp.arange(TAPS, dtype=jnp.int32) - HALF
    inband = jnp.abs(offsets)[None, None, :] <= band_width[:, :, None]
    kinds = jnp.arange(KERNELS, dtype=jnp.int32)
    picked = (basis_index[:, None] == kinds[None, :, None, None]) & inband[:, None]
    return jnp.where(picked, psi_value[:, None], jnp.zeros((), BF16))


def local_taps(psi_value, basis_index, band_width, first_row, rows):
    value_pad = jnp.pad(psi_value, ((1, 1), (0, 0), (0, 0)))
    basis_pad = jnp.pad(basis_index, ((1, 1), (0, 0), (0, 0)))
    width_pad = jnp.pad(band_width, ((1, 1), (0, 0)))
    near = coefficients(
        lax.dynamic_slice_in_dim(value_pad, first_row, rows + 2, 0),
        lax.dynamic_slice_in_dim(basis_pad, first_row, rows + 2, 0),
        lax.dynamic_slice_in_dim(width_pad, first_row, rows + 2, 0),
    )
    direct = near[1 : rows + 1]
    adjoint = jnp.stack(
        [near[offset : offset + rows, :, 2 - offset, ::-1] for offset in range(3)], axis=2
    )
    return direct, adjoint


def halves(part, bit):
    size = part.shape[0] // 2
    keep = lax.dynamic_slice_in_dim(part, bit * size, size, 0)
    give = lax.dynamic_slice_in_dim(part, (1 - bit) * size, size, 0)
    return keep, give


def joined(own, other, bit):
    return jnp.where(
        bit == 0, jnp.concatenate([own, other], 0), jnp.concatenate([other, own], 0)
    )


def summed(keep, give):
    kinds, half, channels = keep.shape
    swap = [(0, 1), (1, 0)]
    part = keep + lax.ppermute(give, "lon", swap).astype(F32)
    part = part.reshape(kinds * half, channels)
    count, step, stages = lax.axis_size("lat"), 1, []
    while step < count:
        pairs = [(i, i ^ step) for i in range(count)]
        stages.append((pairs, (lax.axis_index("lat") // step) % 2))
        step *= 2
    for pairs, bit in stages:
        keep, give = halves(part, bit)
        part = keep + lax.ppermute(give.astype(BF16), "lat", pairs).astype(F32)
    part = part.astype(BF16)
    for pairs, bit in reversed(stages):
        part = joined(part, lax.ppermute(part, "lat", pairs), bit)
    own = part.reshape(kinds, half, channels)
    other = lax.ppermute(own, "lon", swap)
    first = lax.axis_index("lon") == 0
    low, high = jnp.where(first, own, other), jnp.where(first, other, own)
    return jnp.concatenate([low, high], axis=1).astype(F32)


def on_device(activations, cotangent, mixing, psi_value, basis_index, band_width):
    channels, rows, columns = activations.shape
    total_rows = lax.axis_size("lat") * rows
    first_row = lax.axis_index("lat") * rows
    field = activations.transpose(1, 2, 0)
    upstream = cotangent.transpose(1, 2, 0)
    near = halos(field)
    direct, adjoint = local_taps(psi_value, basis_index, band_width, first_row, rows)
    direct_tables, adjoint_tables = banded_tables(direct), banded_tables(adjoint)
    to_hidden = mixing.transpose(0, 2, 1).reshape(KERNELS * channels, channels)
    to_input = mixing.reshape(KERNELS * channels, channels)
    block_out, slope, keep, give = forward(
        field, *near, direct_tables, to_hidden, upstream, 1.0 / total_rows
    )
    grad_mixing = summed(keep, give)
    grad_input = backward(slope, *halos(slope), adjoint_tables, to_input, upstream)
    return block_out.transpose(2, 0, 1), grad_input.transpose(2, 0, 1), grad_mixing


def solution(mesh):
    in_specs = (P("member", "lat", "lon"), P("member", "lat", "lon"), P(), P(), P(), P())
    out_specs = (P("member", "lat", "lon"), P("member", "lat", "lon"), P("member", None, None))
    return jax.shard_map(
        on_device, mesh=mesh, in_specs=in_specs, out_specs=out_specs, check_vma=False
    )
```

```python
import math

import jax
import jax.numpy as jnp
from jax import lax
from jax.experimental import pallas as pl
from jax.experimental.pallas import tpu as pltpu
from jax.sharding import PartitionSpec as P

KERNELS = 9
HALF = 16
TAPS = 2 * HALF + 1
BLK = 128
WIN = BLK + 2 * HALF
DEPTH = 512
VMEM = pl.BlockSpec(memory_space=pltpu.VMEM)
FORWARD_MIB, BACKWARD_MIB = 14, 8


def ORDER(stages):
    return stages


BF16, F32 = jnp.bfloat16, jnp.float32


def call(kernel, out_shape, scratch, flops, size, *operands, name, limit):
    return pl.pallas_call(
        kernel,
        out_shape=out_shape,
        in_specs=[VMEM] * len(operands),
        out_specs=jax.tree.map(lambda _: VMEM, out_shape),
        scratch_shapes=scratch,
        compiler_params=pltpu.CompilerParams(vmem_limit_bytes=limit * 2**20),
        cost_estimate=pl.CostEstimate(flops=flops, bytes_accessed=size, transcendentals=0),
        name=name,
    )(*operands)


def tables_kernel(lines_ref, out_ref):
    rows = lines_ref.shape[0]
    for row in range(rows):
        for kind in range(KERNELS):
            line = jnp.broadcast_to(lines_ref[row, kind : kind + 1, :], (BLK, DEPTH))
            out_ref[row, kind * BLK : (kind + 1) * BLK, :] = pltpu.roll(
                line, 0, 1, stride=1, stride_axis=0
            ).astype(BF16)


def banded_tables(taps):
    lead = taps.shape[0]
    lines = jnp.pad(taps.astype(F32), ((0, 0), (0, 0), (0, 0), (0, WIN - TAPS)))
    lines = jnp.pad(lines.reshape(lead, KERNELS, 3 * WIN), ((0, 0), (0, 0), (0, DEPTH - 3 * WIN)))
    shape = jax.ShapeDtypeStruct((lead, KERNELS * BLK, DEPTH), BF16)
    return call(tables_kernel, shape, [], 0, 6_000_000, lines, name="tables", limit=8)


def starts_of(columns):
    return [min(b * BLK, columns - BLK) for b in range(-(-columns // BLK))]


def banded_row(table_ref, index, wide_refs, buffer_ref, base, columns, channels):
    for start in starts_of(columns):
        window = jnp.concatenate([ref[start : start + WIN] for ref in wide_refs], axis=0)
        for kind in range(KERNELS):
            out = jnp.dot(
                table_ref[index, kind * BLK : (kind + 1) * BLK, : 3 * WIN],
                window,
                preferred_element_type=F32,
            )
            buffer_ref[
                base + start : base + start + BLK, kind * channels : (kind + 1) * channels
            ] = out.astype(BF16)


def gelu_parts(hidden):
    cdf = 0.5 * (1.0 + lax.erf(hidden * (1.0 / math.sqrt(2.0))))
    slope = cdf + hidden * jnp.exp(-0.5 * hidden * hidden) * (1.0 / math.sqrt(2.0 * math.pi))
    return hidden * cdf, slope


def forward_kernel(
    scale, own_ref, lon_ref, above_ref, below_ref, corner_above_ref, corner_below_ref,
    table_ref, mix_ref, cot_ref,
    out_ref, slope_ref, keep_ref, give_ref, wide_ref, buffer_ref, turned_ref,
):
    rows, columns, channels = own_ref.shape
    for row in range(-1, rows + 1):
        if row < 0:
            middle, edges = above_ref[0], corner_above_ref[0]
        elif row == rows:
            middle, edges = below_ref[0], corner_below_ref[0]
        else:
            middle, edges = own_ref[row], lon_ref[row]
        wide_ref[row + 1, 0:HALF] = edges[0:HALF]
        wide_ref[row + 1, HALF : HALF + columns] = middle
        wide_ref[row + 1, HALF + columns :] = edges[HALF:]
    for row in range(rows):
        refs = [wide_ref.at[row + offset] for offset in range(3)]
        banded_row(table_ref, row, refs, buffer_ref, row * columns, columns, channels)
    step = 240
    for row in range(rows):
        for start in range(0, columns, step):
            at = row * columns + start
            hidden = jnp.dot(
                buffer_ref[at : at + step, :], mix_ref[...], preferred_element_type=F32
            )
            value, derivative = gelu_parts(hidden)
            part = slice(start, start + step)
            out_ref[row, part] = (own_ref[row, part].astype(F32) + value).astype(BF16)
            slope = (cot_ref[row, part].astype(F32) * derivative).astype(BF16)
            slope_ref[row, part] = slope
        turned_ref[:, row * columns : (row + 1) * columns] = slope_ref[row].T
    first = lax.axis_index("lon") == 0
    half = channels // 2
    for kind in range(KERNELS):
        grad = scale * jnp.dot(
            turned_ref[...],
            buffer_ref[:, kind * channels : (kind + 1) * channels],
            preferred_element_type=F32,
        )
        low, high = grad[:half], grad[half:]
        part = slice(kind * half, (kind + 1) * half)
        keep_ref[part] = jnp.where(first, low, high)
        give_ref[part] = jnp.where(first, high, low).astype(BF16)
    base = KERNELS * half
    for row in range(rows):
        give_ref[base : base + HALF] = slope_ref[row, columns - HALF :]
        give_ref[base + HALF : base + 2 * HALF] = slope_ref[row, :HALF]
        base += 2 * HALF


def backward_kernel(
    row, above_ref, own_ref, below_ref, table_ref, mix_ref, cot_ref, out_ref, buffer_ref
):
    rows, columns, channels = cot_ref.shape
    refs = []
    for at in range(row - 1, row + 2):
        if at < 0:
            refs.append(above_ref.at[0])
        elif at == rows:
            refs.append(below_ref.at[0])
        else:
            refs.append(own_ref.at[at])
    banded_row(table_ref, rows + row, refs, buffer_ref, 0, columns, channels)
    step = 240
    for start in range(0, columns, step):
        grad = jnp.dot(
            buffer_ref[start : start + step, :], mix_ref[...], preferred_element_type=F32
        )
        part = slice(start, start + step)
        out_ref[0, part] = (cot_ref[row, part].astype(F32) + grad).astype(BF16)


def forward(field, near, table, mix, upstream, scale):
    rows, columns, channels = field.shape
    half = KERNELS * channels // 2
    shapes = (
        jax.ShapeDtypeStruct(field.shape, BF16),
        jax.ShapeDtypeStruct(field.shape, BF16),
        jax.ShapeDtypeStruct((half, channels), F32),
        jax.ShapeDtypeStruct((half + 2 * HALF * rows, channels), BF16),
    )
    scratch = [
        pltpu.VMEM((rows + 2, columns + 2 * HALF, channels), BF16),
        pltpu.VMEM((rows * columns, KERNELS * channels), BF16),
        pltpu.VMEM((channels, rows * columns), BF16),
    ]

    def kernel(*refs):
        forward_kernel(scale, *refs)

    return call(
        kernel, shapes, scratch, 7 * 10**9, 8 * 10**6,
        field, *near, table, mix, upstream, name="forward", limit=FORWARD_MIB,
    )


def backward(row, above, wide, below, table, mix, upstream):
    rows, columns, channels = upstream.shape

    def kernel(*refs):
        backward_kernel(row, *refs)

    return call(
        kernel, jax.ShapeDtypeStruct((1, columns, channels), BF16),
        [pltpu.VMEM((columns, KERNELS * channels), BF16)],
        25 * 10**8, 4 * 10**6, above, wide, below, table, mix, upstream,
        name="backward", limit=BACKWARD_MIB,
    )


SWAP = [(0, 1), (1, 0)]


def shifts(count):
    down = [(i, i + 1) for i in range(count - 1)]
    return down, [(target, source) for source, target in down]


def lat_halo(wide):
    down, up = shifts(lax.axis_size("lat"))
    return lax.ppermute(wide[-1:], "lat", down), lax.ppermute(wide[:1], "lat", up)


def field_halo(field, table):
    down, up = shifts(lax.axis_size("lat"))
    edges = jnp.concatenate([field[:, -HALF:], field[:, :HALF]], axis=1)
    above, below = lat_halo(field)
    edges, table = lax.optimization_barrier((edges, table))
    lon = lax.ppermute(edges, "lon", SWAP)

    def across(pairs):
        return [(2 * a + c, 2 * b + 1 - c) for a, b in pairs for c in range(2)]

    corner_above = lax.ppermute(edges[-1:], ("lat", "lon"), across(down))
    corner_below = lax.ppermute(edges[:1], ("lat", "lon"), across(up))
    return (lon, above, below, corner_above, corner_below), table


def coefficients(psi_value, basis_index, band_width):
    offsets = jnp.arange(TAPS, dtype=jnp.int32) - HALF
    inband = jnp.abs(offsets)[None, None, :] <= band_width[:, :, None]
    kinds = jnp.arange(KERNELS, dtype=jnp.int32)
    picked = (basis_index[:, None] == kinds[None, :, None, None]) & inband[:, None]
    return jnp.where(picked, psi_value[:, None], jnp.zeros((), BF16))


def local_taps(psi_value, basis_index, band_width, first_row, rows):
    value_pad = jnp.pad(psi_value, ((1, 1), (0, 0), (0, 0)))
    basis_pad = jnp.pad(basis_index, ((1, 1), (0, 0), (0, 0)))
    width_pad = jnp.pad(band_width, ((1, 1), (0, 0)))
    near = coefficients(
        lax.dynamic_slice_in_dim(value_pad, first_row, rows + 2, 0),
        lax.dynamic_slice_in_dim(basis_pad, first_row, rows + 2, 0),
        lax.dynamic_slice_in_dim(width_pad, first_row, rows + 2, 0),
    )
    direct = near[1 : rows + 1]
    adjoint = jnp.stack(
        [near[offset : offset + rows, :, 2 - offset, ::-1] for offset in range(3)], axis=2
    )
    return jnp.concatenate([direct, adjoint], axis=0)


def halves(part, bit):
    size = part.shape[0] // 2
    keep = lax.dynamic_slice_in_dim(part, bit * size, size, 0)
    give = lax.dynamic_slice_in_dim(part, (1 - bit) * size, size, 0)
    return keep, give


def joined(own, other, bit):
    return jnp.where(
        bit == 0, jnp.concatenate([own, other], 0), jnp.concatenate([other, own], 0)
    )


def lat_stages():
    count, step, stages = lax.axis_size("lat"), 1, []
    while step < count:
        pairs = [(i, i ^ step) for i in range(count)]
        stages.append((pairs, (lax.axis_index("lat") // step) % 2))
        step *= 2
    return ORDER(stages)


def lat_sum(part, wide):
    stages = lat_stages()
    for at, (pairs, bit) in enumerate(stages[:-1]):
        keep, give = halves(part, bit)
        got = lax.ppermute(give.astype(BF16), "lat", pairs)
        if at == 0:
            got, wide = lax.optimization_barrier((got, wide))
        part = keep + got.astype(F32)
    own = part.astype(BF16)
    other = lax.ppermute(own, "lat", stages[-1][0])
    part = (own.astype(F32) + other.astype(F32)).astype(BF16)
    for pairs, bit in reversed(stages[:-1]):
        part = joined(part, lax.ppermute(part, "lat", pairs), bit)
    return part, wide


def on_device(activations, cotangent, mixing, psi_value, basis_index, band_width):
    channels, rows, columns = activations.shape
    total_rows = lax.axis_size("lat") * rows
    first_row = lax.axis_index("lat") * rows
    half = channels // 2
    field = activations.transpose(1, 2, 0)
    upstream = cotangent.transpose(1, 2, 0)
    table = banded_tables(local_taps(psi_value, basis_index, band_width, first_row, rows))
    near, table = field_halo(field, table)
    to_hidden = mixing.transpose(0, 2, 1).reshape(KERNELS * channels, channels)
    to_input = mixing.reshape(KERNELS * channels, channels)
    block_out, slope, keep, give = forward(
        field, near, table, to_hidden, upstream, 1.0 / total_rows
    )
    got = lax.ppermute(give, "lon", SWAP)
    lon = got[KERNELS * half :].reshape(rows, 2 * HALF, channels)
    wide = jnp.concatenate([lon[:, :HALF], slope, lon[:, HALF:]], axis=1)
    own, wide = lat_sum(keep + got[: KERNELS * half].astype(F32), wide)
    own = own.reshape(KERNELS, half, channels)
    above, below = lat_halo(wide)
    grad_input = jnp.concatenate(
        [backward(row, above, wide, below, table, to_input, upstream) for row in range(rows)], 0
    )
    own, grad_input = lax.optimization_barrier((own, grad_input))
    other = lax.ppermute(own, "lon", SWAP)
    first = lax.axis_index("lon") == 0
    low, high = jnp.where(first, own, other), jnp.where(first, other, own)
    grad_mixing = jnp.concatenate([low, high], axis=1).astype(F32)
    return block_out.transpose(2, 0, 1), grad_input.transpose(2, 0, 1), grad_mixing


def solution(mesh):
    in_specs = (P("member", "lat", "lon"), P("member", "lat", "lon"), P(), P(), P(), P())
    out_specs = (P("member", "lat", "lon"), P("member", "lat", "lon"), P("member", None, None))
    return jax.shard_map(
        on_device, mesh=mesh, in_specs=in_specs, out_specs=out_specs, check_vma=False
    )
```

```python
import math

import jax
import jax.numpy as jnp
from jax import lax
from jax.experimental import pallas as pl
from jax.experimental.pallas import tpu as pltpu
from jax.sharding import PartitionSpec as P

KERNELS = 9
HALF = 16
TAPS = 2 * HALF + 1
BLK = 128
WIN = BLK + 2 * HALF
DEPTH = 512
STEP = 240
SWAP = [(0, 1), (1, 0)]
VMEM = pl.BlockSpec(memory_space=pltpu.VMEM)
BF16, F32 = jnp.bfloat16, jnp.float32


def call(kernel, out_shape, scratch, flops, size, *operands, name, limit):
    return pl.pallas_call(
        kernel,
        out_shape=out_shape,
        in_specs=[VMEM] * len(operands),
        out_specs=jax.tree.map(lambda _: VMEM, out_shape),
        scratch_shapes=scratch,
        compiler_params=pltpu.CompilerParams(vmem_limit_bytes=limit * 2**20),
        cost_estimate=pl.CostEstimate(flops=flops, bytes_accessed=size, transcendentals=0),
        name=name,
    )(*operands)


def tables_kernel(lines_ref, mixing_ref, turned_ref, *out_refs):
    channels = mixing_ref.shape[2]
    for kind in range(KERNELS):
        turned_ref[kind * channels : (kind + 1) * channels] = mixing_ref[kind].T
    for row, out_ref in enumerate(out_refs):
        for kind in range(KERNELS):
            line = jnp.broadcast_to(lines_ref[row, kind : kind + 1, :], (BLK, DEPTH))
            out_ref[kind * BLK : (kind + 1) * BLK, :] = pltpu.roll(
                line, 0, 1, stride=1, stride_axis=0
            ).astype(BF16)


def banded_tables(taps, mixing):
    lead = taps.shape[0]
    kinds, channels, _ = mixing.shape
    lines = jnp.pad(taps.astype(F32), ((0, 0), (0, 0), (0, 0), (0, WIN - TAPS)))
    lines = jnp.pad(lines.reshape(lead, KERNELS, 3 * WIN), ((0, 0), (0, 0), (0, DEPTH - 3 * WIN)))
    turned = jax.ShapeDtypeStruct((kinds * channels, channels), BF16)
    shapes = [turned] + [jax.ShapeDtypeStruct((KERNELS * BLK, DEPTH), BF16)] * lead
    return call(
        tables_kernel, shapes, [], 10**7, 3_000_000, lines, mixing, name="tables", limit=12
    )


def parity():
    return lax.rem(lax.axis_index("lat"), 2)


def place(wide_ref, slot, middle, edges):
    columns = middle.shape[0]
    wide_ref[slot, 0:HALF] = edges[0:HALF]
    wide_ref[slot, HALF : HALF + columns] = middle
    wide_ref[slot, HALF + columns :] = edges[HALF:]


def banded_row(table_ref, wide_ref, buffer_ref):
    columns = buffer_ref.shape[0]
    channels = wide_ref.shape[2]
    for block in range(-(-columns // BLK)):
        start = min(block * BLK, columns - BLK)
        window = jnp.concatenate(
            [wide_ref[offset, start : start + WIN] for offset in range(3)], axis=0
        )
        for kind in range(KERNELS):
            out = jnp.dot(
                table_ref[kind * BLK : (kind + 1) * BLK, : 3 * WIN],
                window,
                preferred_element_type=F32,
            )
            buffer_ref[start : start + BLK, kind * channels : (kind + 1) * channels] = (
                out.astype(BF16)
            )


def gelu_parts(hidden):
    cdf = 0.5 * (1.0 + lax.erf(hidden * (1.0 / math.sqrt(2.0))))
    slope = cdf + hidden * jnp.exp(-0.5 * hidden * hidden) * (1.0 / math.sqrt(2.0 * math.pi))
    return hidden * cdf, slope


def gelu_row(field_ref, cot_ref, row, mix_ref, buffer_ref, out_ref, slope_ref, turned_ref):
    columns = buffer_ref.shape[0]
    for start in range(0, columns, STEP):
        part = slice(start, start + STEP)
        hidden = jnp.dot(buffer_ref[part, :], mix_ref[...], preferred_element_type=F32)
        value, derivative = gelu_parts(hidden)
        out_ref[part] = (field_ref[row, part].astype(F32) + value).astype(BF16)
        slope_ref[part] = (cot_ref[row, part].astype(F32) * derivative).astype(BF16)
    turned_ref[...] = slope_ref[...].T


def grad_of(turned_ref, buffer_ref, kind):
    channels = turned_ref.shape[0]
    return jnp.dot(
        turned_ref[...],
        buffer_ref[:, kind * channels : (kind + 1) * channels],
        preferred_element_type=F32,
    )


def near_kernel(
    field_ref, lon_ref, row_ref, edge_ref, table_ref, mix_ref, cot_ref,
    out_ref, slope_ref, edges_ref, grad_ref, wide_ref, buffer_ref, turned_ref,
):
    odd = parity()
    near, far = 1 - odd, odd
    place(wide_ref, 2 * odd, field_ref[far], lon_ref[far])
    place(wide_ref, 1, field_ref[near], lon_ref[near])
    place(wide_ref, 2 - 2 * odd, row_ref[0], edge_ref[0])
    banded_row(table_ref, wide_ref, buffer_ref)
    gelu_row(field_ref, cot_ref, near, mix_ref, buffer_ref, out_ref, slope_ref, turned_ref)
    columns = slope_ref.shape[0]
    edges_ref[0, :HALF] = slope_ref[columns - HALF :]
    edges_ref[0, HALF:] = slope_ref[:HALF]
    channels = turned_ref.shape[0]
    for kind in range(KERNELS):
        grad_ref[kind * channels : (kind + 1) * channels] = grad_of(turned_ref, buffer_ref, kind)


def far_kernel(
    scale, field_ref, lon_ref, row_ref, table_ref, mix_ref, cot_ref,
    near_out_ref, grad_ref,
    out_ref, slope_ref, keep_ref, give_ref, wide_ref, buffer_ref, turned_ref,
):
    odd = parity()
    near, far = 1 - odd, odd
    place(wide_ref, 2 - 2 * odd, field_ref[near], lon_ref[near])
    place(wide_ref, 1, field_ref[far], lon_ref[far])
    wide_ref[2 * odd] = row_ref[0]
    banded_row(table_ref, wide_ref, buffer_ref)
    gelu_row(
        field_ref, cot_ref, far, mix_ref, buffer_ref, out_ref.at[far], slope_ref, turned_ref
    )
    out_ref[near] = near_out_ref[...]
    first = lax.axis_index("lon") == 0
    columns = slope_ref.shape[0]
    channels = turned_ref.shape[0]
    half = channels // 2
    for kind in range(KERNELS):
        whole = slice(kind * channels, (kind + 1) * channels)
        grad = scale * (grad_of(turned_ref, buffer_ref, kind) + grad_ref[whole])
        low, high = grad[:half], grad[half:]
        part = slice(kind * half, (kind + 1) * half)
        keep_ref[part] = jnp.where(first, low, high)
        give_ref[part] = jnp.where(first, high, low).astype(BF16)
    base = KERNELS * half
    give_ref[base : base + HALF] = slope_ref[columns - HALF :]
    give_ref[base + HALF : base + 2 * HALF] = slope_ref[:HALF]


def contract_row(cot_ref, row, mix_ref, buffer_ref, out_ref):
    columns = buffer_ref.shape[0]
    for start in range(0, columns, STEP):
        part = slice(start, start + STEP)
        grad = jnp.dot(buffer_ref[part, :], mix_ref[...], preferred_element_type=F32)
        out_ref[part] = (cot_ref[row, part].astype(F32) + grad).astype(BF16)


def back_near_kernel(
    near_ref, far_ref, row_ref, table_ref, mix_ref, cot_ref, out_ref, wide_ref, buffer_ref
):
    odd = parity()
    wide_ref[2 * odd] = far_ref[0]
    wide_ref[1] = near_ref[0]
    wide_ref[2 - 2 * odd] = row_ref[0]
    banded_row(table_ref, wide_ref, buffer_ref)
    contract_row(cot_ref, 1 - odd, mix_ref, buffer_ref, out_ref)


def back_far_kernel(
    near_ref, far_ref, row_ref, table_ref, mix_ref, cot_ref, near_out_ref,
    out_ref, wide_ref, buffer_ref,
):
    odd = parity()
    wide_ref[2 - 2 * odd] = near_ref[0]
    wide_ref[1] = far_ref[0]
    wide_ref[2 * odd] = row_ref[0]
    banded_row(table_ref, wide_ref, buffer_ref)
    contract_row(cot_ref, odd, mix_ref, buffer_ref, out_ref.at[odd])
    out_ref[1 - odd] = near_out_ref[...]


def lat_bit_clear(step):
    return lax.rem(lax.div(lax.axis_index("lat"), step), 2) == 0


def first_split_kernel(
    step, keep_ref, got_ref, slope_ref, mine_ref, give_ref, wide_ref
):
    rows = keep_ref.shape[0]
    split_kernel(step, keep_ref, got_ref, mine_ref, give_ref)
    columns = slope_ref.shape[0]
    wide_ref[0, :HALF] = got_ref[rows : rows + HALF]
    wide_ref[0, HALF : HALF + columns] = slope_ref[...]
    wide_ref[0, HALF + columns :] = got_ref[rows + HALF :]


def split_kernel(step, keep_ref, got_ref, mine_ref, give_ref):
    half = keep_ref.shape[0] // 2
    clear = lat_bit_clear(step)
    low = keep_ref[:half] + got_ref[:half].astype(F32)
    high = keep_ref[half:] + got_ref[half : 2 * half].astype(F32)
    mine_ref[...] = jnp.where(clear, low, high)
    give_ref[...] = jnp.where(clear, high, low).astype(BF16)


def join_kernel(step, own_ref, got_ref, out_ref):
    half = own_ref.shape[0]
    clear = lat_bit_clear(step)
    out_ref[:half] = jnp.where(clear, own_ref[...], got_ref[...])
    out_ref[half:] = jnp.where(clear, got_ref[...], own_ref[...])


def round_kernel(keep_ref, got_ref, out_ref):
    out_ref[...] = (keep_ref[...] + got_ref[...].astype(F32)).astype(BF16)


def total_kernel(own_ref, got_ref, out_ref):
    out_ref[...] = (own_ref[...].astype(F32) + got_ref[...].astype(F32)).astype(BF16)


def final_kernel(own_ref, got_ref, out_ref):
    kinds, channels, _ = out_ref.shape
    half = channels // 2
    first = lax.axis_index("lon") == 0
    for kind in range(kinds):
        part = slice(kind * half, (kind + 1) * half)
        own, got = own_ref[part].astype(F32), got_ref[part].astype(F32)
        out_ref[kind, :half] = jnp.where(first, own, got)
        out_ref[kind, half:] = jnp.where(first, got, own)


def glue(kernel, shapes, *operands, name):
    return call(kernel, shapes, [], 10**6, 10**6, *operands, name=name, limit=8)


def tiled(rows):
    return rows % 16 == 0


def bit_of(step):
    return (lax.axis_index("lat") // step) % 2


def split(step, keep, got):
    rows, channels = keep.shape
    if not tiled(rows // 2):
        whole = keep + got.astype(F32)
        mine, give = halves(whole, bit_of(step))
        return mine, give.astype(BF16)

    def kernel(*refs):
        split_kernel(step, *refs)

    shapes = (
        jax.ShapeDtypeStruct((rows // 2, channels), F32),
        jax.ShapeDtypeStruct((rows // 2, channels), BF16),
    )
    return glue(kernel, shapes, keep, got, name="split")


def first_split(step, keep, got, slope):
    rows, channels = keep.shape

    def kernel(*refs):
        first_split_kernel(step, *refs)

    shapes = (
        jax.ShapeDtypeStruct((rows // 2, channels), F32),
        jax.ShapeDtypeStruct((rows // 2, channels), BF16),
        jax.ShapeDtypeStruct((1, slope.shape[0] + 2 * HALF, channels), BF16),
    )
    return glue(kernel, shapes, keep, got, slope, name="first_split")


def join(step, own, got):
    rows, channels = own.shape
    if not tiled(rows):
        return joined(own, got, bit_of(step))

    def kernel(*refs):
        join_kernel(step, *refs)

    return glue(
        kernel, jax.ShapeDtypeStruct((2 * rows, channels), BF16), own, got, name="join"
    )


def added(kernel, own, got):
    if not tiled(own.shape[0]):
        return (own.astype(F32) + got.astype(F32)).astype(BF16)
    return glue(kernel, jax.ShapeDtypeStruct(own.shape, BF16), own, got, name="added")


def scratch_of(columns, channels):
    return [
        pltpu.VMEM((3, columns + 2 * HALF, channels), BF16),
        pltpu.VMEM((columns, KERNELS * channels), BF16),
    ]


def forward_near(field, lon, row, edge, table, mix, upstream):
    _, columns, channels = field.shape
    shapes = (
        jax.ShapeDtypeStruct((columns, channels), BF16),
        jax.ShapeDtypeStruct((columns, channels), BF16),
        jax.ShapeDtypeStruct((1, 2 * HALF, channels), BF16),
        jax.ShapeDtypeStruct((KERNELS * channels, channels), F32),
    )
    turned = pltpu.VMEM((channels, columns), BF16)
    return call(
        near_kernel, shapes, scratch_of(columns, channels) + [turned], 35 * 10**8, 4 * 10**6,
        field, lon, row, edge, table, mix, upstream, name="near", limit=16,
    )


def forward_far(field, lon, row, table, mix, upstream, near_out, grad, scale):
    _, columns, channels = field.shape
    half = KERNELS * channels // 2
    shapes = (
        jax.ShapeDtypeStruct(field.shape, BF16),
        jax.ShapeDtypeStruct((columns, channels), BF16),
        jax.ShapeDtypeStruct((half, channels), F32),
        jax.ShapeDtypeStruct((half + 2 * HALF, channels), BF16),
    )
    turned = pltpu.VMEM((channels, columns), BF16)

    def kernel(*refs):
        far_kernel(scale, *refs)

    return call(
        kernel, shapes, scratch_of(columns, channels) + [turned], 35 * 10**8, 4 * 10**6,
        field, lon, row, table, mix, upstream, near_out, grad,
        name="far", limit=16,
    )


def backward_near(near, far, row, table, mix, upstream):
    _, columns, channels = upstream.shape
    return call(
        back_near_kernel, jax.ShapeDtypeStruct((columns, channels), BF16),
        scratch_of(columns, channels), 25 * 10**8, 3 * 10**6,
        near, far, row, table, mix, upstream, name="back_near", limit=10,
    )


def backward_far(near, far, row, table, mix, upstream, near_out):
    _, columns, channels = upstream.shape
    return call(
        back_far_kernel, jax.ShapeDtypeStruct(upstream.shape, BF16),
        scratch_of(columns, channels), 25 * 10**8, 3 * 10**6,
        near, far, row, table, mix, upstream, near_out, name="back_far", limit=10,
    )


def near_swap(row):
    count = lax.axis_size("lat")
    return lax.ppermute(row, "lat", [(i, i ^ 1) for i in range(count)])


def far_swap(row):
    count = lax.axis_size("lat")
    pairs = [(i, i + 1) for i in range(1, count - 1, 2)]
    return lax.ppermute(row, "lat", pairs + [(b, a) for a, b in pairs])


def edges_of(rows):
    return jnp.concatenate([rows[:, -HALF:], rows[:, :HALF]], axis=1)


def core_swap(rows):
    return lax.ppermute(rows, "lon", SWAP)


def widened(row, edges):
    return jnp.concatenate([edges[:, :HALF], row, edges[:, HALF:]], axis=1)


def coefficients(psi_value, basis_index, band_width):
    offsets = jnp.arange(TAPS, dtype=jnp.int32) - HALF
    inband = jnp.abs(offsets)[None, None, :] <= band_width[:, :, None]
    kinds = jnp.arange(KERNELS, dtype=jnp.int32)
    picked = (basis_index[:, None] == kinds[None, :, None, None]) & inband[:, None]
    return jnp.where(picked, psi_value[:, None], jnp.zeros((), BF16))


def local_taps(psi_value, basis_index, band_width, first_row, rows):
    value_pad = jnp.pad(psi_value, ((1, 1), (0, 0), (0, 0)))
    basis_pad = jnp.pad(basis_index, ((1, 1), (0, 0), (0, 0)))
    width_pad = jnp.pad(band_width, ((1, 1), (0, 0)))
    near = coefficients(
        lax.dynamic_slice_in_dim(value_pad, first_row, rows + 2, 0),
        lax.dynamic_slice_in_dim(basis_pad, first_row, rows + 2, 0),
        lax.dynamic_slice_in_dim(width_pad, first_row, rows + 2, 0),
    )
    direct = near[1 : rows + 1]
    adjoint = jnp.stack(
        [near[offset : offset + rows, :, 2 - offset, ::-1] for offset in range(3)], axis=2
    )
    even = parity() == 0
    return jnp.concatenate(
        [jnp.where(even, taps[::-1], taps) for taps in (direct, adjoint)], axis=0
    )


def halves(part, bit):
    size = part.shape[0] // 2
    keep = lax.dynamic_slice_in_dim(part, bit * size, size, 0)
    give = lax.dynamic_slice_in_dim(part, (1 - bit) * size, size, 0)
    return keep, give


def joined(own, other, bit):
    return jnp.where(
        bit == 0, jnp.concatenate([own, other], 0), jnp.concatenate([other, own], 0)
    )


def lat_swap(rows, step):
    return lax.ppermute(rows, "lat", [(i, i ^ step) for i in range(lax.axis_size("lat"))])


def on_device(activations, cotangent, mixing, psi_value, basis_index, band_width):
    channels, rows, columns = activations.shape
    total_rows = lax.axis_size("lat") * rows
    first_row = lax.axis_index("lat") * rows
    half = channels // 2
    far_row = parity()
    field = activations.transpose(1, 2, 0)
    upstream = cotangent.transpose(1, 2, 0)
    to_input = mixing.reshape(KERNELS * channels, channels)

    near_halo = near_swap(lax.dynamic_slice_in_dim(field, 1 - far_row, 1, 0))
    lon = core_swap(edges_of(field))
    far_own = widened(
        lax.dynamic_slice_in_dim(field, far_row, 1, 0),
        lax.dynamic_slice_in_dim(lon, far_row, 1, 0),
    )
    to_hidden, *tables = banded_tables(
        local_taps(psi_value, basis_index, band_width, first_row, rows), mixing
    )
    near_halo, far_own, to_hidden, *tables = lax.optimization_barrier(
        (near_halo, far_own, to_hidden, *tables)
    )
    far_halo = far_swap(far_own)
    near_edges = core_swap(edges_of(near_halo))
    near_out, near_slope, slope_edges, grad = forward_near(
        field, lon, near_halo, near_edges, tables[0], to_hidden, upstream
    )
    near_wide = widened(near_slope[None], core_swap(slope_edges))
    near_slope_halo = near_swap(near_wide)
    block_out, far_slope, keep, give = forward_far(
        field, lon, far_halo, tables[1], to_hidden, upstream, near_out, grad, 1.0 / total_rows
    )
    steps = [2**at for at in range((lax.axis_size("lat") - 1).bit_length())]
    mine, give, far_wide = first_split(steps[0], keep, core_swap(give), far_slope)
    got = lat_swap(give, steps[0])
    near_grad = backward_near(
        near_wide, far_wide, near_slope_halo, tables[2], to_input, upstream
    )
    got, far_wide, near_grad = lax.optimization_barrier((got, far_wide, near_grad))
    for at, step in enumerate(steps[1:-1]):
        mine, give = split(step, mine, got)
        got = lat_swap(give, step)
    own = added(round_kernel, mine, got)
    own = added(total_kernel, own, lat_swap(own, steps[-1]))
    far_slope_halo = far_swap(far_wide)
    for step in reversed(steps[:-1]):
        own = join(step, own, lat_swap(own, step))
    grad_input = backward_far(
        near_wide, far_wide, far_slope_halo, tables[3], to_input, upstream, near_grad
    )
    own, grad_input = lax.optimization_barrier((own, grad_input))
    grad_mixing = glue(
        final_kernel, jax.ShapeDtypeStruct(mixing.shape, F32), own, core_swap(own), name="final"
    )
    return block_out.transpose(2, 0, 1), grad_input.transpose(2, 0, 1), grad_mixing


def solution(mesh):
    in_specs = (P("member", "lat", "lon"), P("member", "lat", "lon"), P(), P(), P(), P())
    out_specs = (P("member", "lat", "lon"), P("member", "lat", "lon"), P("member", None, None))
    return jax.shard_map(
        on_device, mesh=mesh, in_specs=in_specs, out_specs=out_specs, check_vma=False
    )
```

```python
import math

import jax
import jax.numpy as jnp
from jax import lax
from jax.experimental import pallas as pl
from jax.experimental.pallas import tpu as pltpu
from jax.sharding import PartitionSpec as P

KERNELS = 9
HALF = 16
TAPS = 2 * HALF + 1
BLK = 128
WIN = BLK + 2 * HALF
DEPTH = 512
STEP = 240
SWAP = [(0, 1), (1, 0)]
VMEM = pl.BlockSpec(memory_space=pltpu.VMEM)
BF16, F32 = jnp.bfloat16, jnp.float32


def call(kernel, out_shape, scratch, flops, size, *operands, name, limit):
    return pl.pallas_call(
        kernel,
        out_shape=out_shape,
        in_specs=[VMEM] * len(operands),
        out_specs=jax.tree.map(lambda _: VMEM, out_shape),
        scratch_shapes=scratch,
        compiler_params=pltpu.CompilerParams(vmem_limit_bytes=limit * 2**20),
        cost_estimate=pl.CostEstimate(flops=flops, bytes_accessed=size, transcendentals=0),
        name=name,
    )(*operands)


def tables_kernel(lines_ref, mixing_ref, turned_ref, *out_refs):
    channels = mixing_ref.shape[2]
    for kind in range(KERNELS):
        turned_ref[kind * channels : (kind + 1) * channels] = mixing_ref[kind].T
    for row, out_ref in enumerate(out_refs):
        for kind in range(KERNELS):
            line = jnp.broadcast_to(lines_ref[row, kind : kind + 1, :], (BLK, DEPTH))
            out_ref[kind * BLK : (kind + 1) * BLK, :] = pltpu.roll(
                line, 0, 1, stride=1, stride_axis=0
            ).astype(BF16)


def banded_tables(taps, mixing):
    lead = taps.shape[0]
    kinds, channels, _ = mixing.shape
    lines = jnp.pad(taps.astype(F32), ((0, 0), (0, 0), (0, 0), (0, WIN - TAPS)))
    lines = jnp.pad(lines.reshape(lead, KERNELS, 3 * WIN), ((0, 0), (0, 0), (0, DEPTH - 3 * WIN)))
    turned = jax.ShapeDtypeStruct((kinds * channels, channels), BF16)
    shapes = [turned] + [jax.ShapeDtypeStruct((KERNELS * BLK, DEPTH), BF16)] * lead
    return call(
        tables_kernel, shapes, [], 10**7, 3_000_000, lines, mixing, name="tables", limit=12
    )


def parity():
    return lax.rem(lax.axis_index("lat"), 2)


def place(wide_ref, slot, middle, edges):
    columns = middle.shape[0]
    wide_ref[slot, 0:HALF] = edges[0:HALF]
    wide_ref[slot, HALF : HALF + columns] = middle
    wide_ref[slot, HALF + columns :] = edges[HALF:]


def banded_row(table_ref, wide_ref, buffer_ref):
    columns = buffer_ref.shape[0]
    channels = wide_ref.shape[2]
    for block in range(-(-columns // BLK)):
        start = min(block * BLK, columns - BLK)
        window = jnp.concatenate(
            [wide_ref[offset, start : start + WIN] for offset in range(3)], axis=0
        )
        for kind in range(KERNELS):
            out = jnp.dot(
                table_ref[kind * BLK : (kind + 1) * BLK, : 3 * WIN],
                window,
                preferred_element_type=F32,
            )
            buffer_ref[start : start + BLK, kind * channels : (kind + 1) * channels] = (
                out.astype(BF16)
            )


def gelu_parts(hidden):
    cdf = 0.5 * (1.0 + lax.erf(hidden * (1.0 / math.sqrt(2.0))))
    slope = cdf + hidden * jnp.exp(-0.5 * hidden * hidden) * (1.0 / math.sqrt(2.0 * math.pi))
    return hidden * cdf, slope


def gelu_row(field_ref, cot_ref, row, mix_ref, buffer_ref, out_ref, slope_ref, turned_ref):
    columns = buffer_ref.shape[0]
    for start in range(0, columns, STEP):
        part = slice(start, start + STEP)
        hidden = jnp.dot(buffer_ref[part, :], mix_ref[...], preferred_element_type=F32)
        value, derivative = gelu_parts(hidden)
        out_ref[part] = (field_ref[row, part].astype(F32) + value).astype(BF16)
        slope_ref[part] = (cot_ref[row, part].astype(F32) * derivative).astype(BF16)
    turned_ref[...] = slope_ref[...].T


def grad_of(turned_ref, buffer_ref, kind):
    channels = turned_ref.shape[0]
    return jnp.dot(
        turned_ref[...],
        buffer_ref[:, kind * channels : (kind + 1) * channels],
        preferred_element_type=F32,
    )


def first_kernel(
    field_ref, lon_ref, row_ref, edge_ref, table_ref, mix_ref, cot_ref,
    out_ref, slope_ref, grad_ref, wide_ref, buffer_ref, turned_ref,
):
    odd = parity()
    near, far = 1 - odd, odd
    place(wide_ref, 2 - 2 * odd, field_ref[near], lon_ref[near])
    place(wide_ref, 1, field_ref[far], lon_ref[far])
    place(wide_ref, 2 * odd, row_ref[0], edge_ref[0])
    banded_row(table_ref, wide_ref, buffer_ref)
    gelu_row(field_ref, cot_ref, far, mix_ref, buffer_ref, out_ref, slope_ref, turned_ref)
    channels = turned_ref.shape[0]
    for kind in range(KERNELS):
        grad_ref[kind * channels : (kind + 1) * channels] = grad_of(turned_ref, buffer_ref, kind)


def second_kernel(
    scale, field_ref, lon_ref, row_ref, table_ref, mix_ref, cot_ref,
    far_out_ref, far_slope_ref, grad_ref,
    out_ref, slope_ref, keep_ref, give_ref, wide_ref, buffer_ref, turned_ref,
):
    odd = parity()
    near, far = 1 - odd, odd
    place(wide_ref, 2 * odd, field_ref[far], lon_ref[far])
    place(wide_ref, 1, field_ref[near], lon_ref[near])
    wide_ref[2 - 2 * odd] = row_ref[0]
    banded_row(table_ref, wide_ref, buffer_ref)
    gelu_row(
        field_ref, cot_ref, near, mix_ref, buffer_ref, out_ref.at[near], slope_ref, turned_ref
    )
    out_ref[far] = far_out_ref[...]
    first = lax.axis_index("lon") == 0
    columns = slope_ref.shape[0]
    channels = turned_ref.shape[0]
    half = channels // 2
    for kind in range(KERNELS):
        whole = slice(kind * channels, (kind + 1) * channels)
        grad = scale * (grad_of(turned_ref, buffer_ref, kind) + grad_ref[whole])
        low, high = grad[:half], grad[half:]
        part = slice(kind * half, (kind + 1) * half)
        keep_ref[part] = jnp.where(first, low, high)
        give_ref[part] = jnp.where(first, high, low).astype(BF16)
    base = KERNELS * half
    for ref in (far_slope_ref, slope_ref):
        give_ref[base : base + HALF] = ref[columns - HALF :]
        give_ref[base + HALF : base + 2 * HALF] = ref[:HALF]
        base += 2 * HALF


def contract_row(cot_ref, row, mix_ref, buffer_ref, out_ref):
    columns = buffer_ref.shape[0]
    for start in range(0, columns, STEP):
        part = slice(start, start + STEP)
        grad = jnp.dot(buffer_ref[part, :], mix_ref[...], preferred_element_type=F32)
        out_ref[part] = (cot_ref[row, part].astype(F32) + grad).astype(BF16)


def back_first_kernel(
    far_ref, near_ref, row_ref, edge_ref, table_ref, mix_ref, cot_ref,
    out_ref, wide_ref, buffer_ref,
):
    odd = parity()
    wide_ref[2 - 2 * odd] = near_ref[0]
    wide_ref[1] = far_ref[0]
    place(wide_ref, 2 * odd, row_ref[0], edge_ref[0])
    banded_row(table_ref, wide_ref, buffer_ref)
    contract_row(cot_ref, odd, mix_ref, buffer_ref, out_ref)


def back_second_kernel(
    far_ref, near_ref, row_ref, table_ref, mix_ref, cot_ref, far_out_ref,
    out_ref, wide_ref, buffer_ref,
):
    odd = parity()
    wide_ref[2 * odd] = far_ref[0]
    wide_ref[1] = near_ref[0]
    wide_ref[2 - 2 * odd] = row_ref[0]
    banded_row(table_ref, wide_ref, buffer_ref)
    contract_row(cot_ref, 1 - odd, mix_ref, buffer_ref, out_ref.at[1 - odd])
    out_ref[odd] = far_out_ref[...]


def lat_bit_clear(step):
    return lax.rem(lax.div(lax.axis_index("lat"), step), 2) == 0


def first_split_kernel(
    step, keep_ref, got_ref, far_ref, near_ref, mine_ref, give_ref, far_wide_ref, near_wide_ref
):
    split_kernel(step, keep_ref, got_ref, mine_ref, give_ref)
    base = keep_ref.shape[0]
    for row_ref, wide_ref in ((far_ref, far_wide_ref), (near_ref, near_wide_ref)):
        columns = row_ref.shape[0]
        wide_ref[0, :HALF] = got_ref[base : base + HALF]
        wide_ref[0, HALF : HALF + columns] = row_ref[...]
        wide_ref[0, HALF + columns :] = got_ref[base + HALF : base + 2 * HALF]
        base += 2 * HALF


def split_kernel(step, keep_ref, got_ref, mine_ref, give_ref):
    half = keep_ref.shape[0] // 2
    clear = lat_bit_clear(step)
    low = keep_ref[:half] + got_ref[:half].astype(F32)
    high = keep_ref[half:] + got_ref[half : 2 * half].astype(F32)
    mine_ref[...] = jnp.where(clear, low, high)
    give_ref[...] = jnp.where(clear, high, low).astype(BF16)


def join_kernel(step, own_ref, got_ref, out_ref):
    half = own_ref.shape[0]
    clear = lat_bit_clear(step)
    out_ref[:half] = jnp.where(clear, own_ref[...], got_ref[...])
    out_ref[half:] = jnp.where(clear, got_ref[...], own_ref[...])


def round_kernel(keep_ref, got_ref, out_ref):
    out_ref[...] = (keep_ref[...] + got_ref[...].astype(F32)).astype(BF16)


def total_kernel(own_ref, got_ref, out_ref):
    out_ref[...] = (own_ref[...].astype(F32) + got_ref[...].astype(F32)).astype(BF16)


def final_kernel(own_ref, got_ref, out_ref):
    kinds, channels, _ = out_ref.shape
    half = channels // 2
    first = lax.axis_index("lon") == 0
    for kind in range(kinds):
        part = slice(kind * half, (kind + 1) * half)
        own, got = own_ref[part].astype(F32), got_ref[part].astype(F32)
        out_ref[kind, :half] = jnp.where(first, own, got)
        out_ref[kind, half:] = jnp.where(first, got, own)


def glue(kernel, shapes, *operands, name):
    return call(kernel, shapes, [], 10**6, 10**6, *operands, name=name, limit=8)


def tiled(rows):
    return rows % 16 == 0


def bit_of(step):
    return (lax.axis_index("lat") // step) % 2


def split(step, keep, got):
    rows, channels = keep.shape
    if not tiled(rows // 2):
        whole = keep + got.astype(F32)
        mine, give = halves(whole, bit_of(step))
        return mine, give.astype(BF16)

    def kernel(*refs):
        split_kernel(step, *refs)

    shapes = (
        jax.ShapeDtypeStruct((rows // 2, channels), F32),
        jax.ShapeDtypeStruct((rows // 2, channels), BF16),
    )
    return glue(kernel, shapes, keep, got, name="split")


def first_split(step, keep, got, far, near):
    rows, channels = keep.shape

    def kernel(*refs):
        first_split_kernel(step, *refs)

    wide = jax.ShapeDtypeStruct((1, far.shape[0] + 2 * HALF, channels), BF16)
    shapes = (
        jax.ShapeDtypeStruct((rows // 2, channels), F32),
        jax.ShapeDtypeStruct((rows // 2, channels), BF16),
        wide,
        wide,
    )
    return glue(kernel, shapes, keep, got, far, near, name="first_split")


def join(step, own, got):
    rows, channels = own.shape
    if not tiled(rows):
        return joined(own, got, bit_of(step))

    def kernel(*refs):
        join_kernel(step, *refs)

    return glue(
        kernel, jax.ShapeDtypeStruct((2 * rows, channels), BF16), own, got, name="join"
    )


def added(kernel, own, got):
    if not tiled(own.shape[0]):
        return (own.astype(F32) + got.astype(F32)).astype(BF16)
    return glue(kernel, jax.ShapeDtypeStruct(own.shape, BF16), own, got, name="added")


def scratch_of(columns, channels):
    return [
        pltpu.VMEM((3, columns + 2 * HALF, channels), BF16),
        pltpu.VMEM((columns, KERNELS * channels), BF16),
    ]


def forward_first(field, lon, row, edge, table, mix, upstream):
    _, columns, channels = field.shape
    shapes = (
        jax.ShapeDtypeStruct((columns, channels), BF16),
        jax.ShapeDtypeStruct((columns, channels), BF16),
        jax.ShapeDtypeStruct((KERNELS * channels, channels), F32),
    )
    turned = pltpu.VMEM((channels, columns), BF16)
    return call(
        first_kernel, shapes, scratch_of(columns, channels) + [turned], 35 * 10**8, 4 * 10**6,
        field, lon, row, edge, table, mix, upstream, name="first", limit=16,
    )


def forward_second(field, lon, row, table, mix, upstream, far_out, far_slope, grad, scale):
    _, columns, channels = field.shape
    half = KERNELS * channels // 2
    shapes = (
        jax.ShapeDtypeStruct(field.shape, BF16),
        jax.ShapeDtypeStruct((columns, channels), BF16),
        jax.ShapeDtypeStruct((half, channels), F32),
        jax.ShapeDtypeStruct((half + 4 * HALF, channels), BF16),
    )
    turned = pltpu.VMEM((channels, columns), BF16)

    def kernel(*refs):
        second_kernel(scale, *refs)

    return call(
        kernel, shapes, scratch_of(columns, channels) + [turned], 35 * 10**8, 4 * 10**6,
        field, lon, row, table, mix, upstream, far_out, far_slope, grad,
        name="second", limit=16,
    )


def backward_first(far, near, row, edge, table, mix, upstream):
    _, columns, channels = upstream.shape
    return call(
        back_first_kernel, jax.ShapeDtypeStruct((columns, channels), BF16),
        scratch_of(columns, channels), 25 * 10**8, 3 * 10**6,
        far, near, row, edge, table, mix, upstream, name="back_first", limit=10,
    )


def backward_second(far, near, row, table, mix, upstream, far_out):
    _, columns, channels = upstream.shape
    return call(
        back_second_kernel, jax.ShapeDtypeStruct(upstream.shape, BF16),
        scratch_of(columns, channels), 25 * 10**8, 3 * 10**6,
        far, near, row, table, mix, upstream, far_out, name="back_second", limit=10,
    )


def near_swap(row):
    count = lax.axis_size("lat")
    return lax.ppermute(row, "lat", [(i, i ^ 1) for i in range(count)])


def far_swap(row):
    count = lax.axis_size("lat")
    pairs = [(i, i + 1) for i in range(1, count - 1, 2)]
    return lax.ppermute(row, "lat", pairs + [(b, a) for a, b in pairs])


def edges_of(rows):
    return jnp.concatenate([rows[:, -HALF:], rows[:, :HALF]], axis=1)


def core_swap(rows):
    return lax.ppermute(rows, "lon", SWAP)


def widened(row, edges):
    return jnp.concatenate([edges[:, :HALF], row, edges[:, HALF:]], axis=1)


def coefficients(psi_value, basis_index, band_width):
    offsets = jnp.arange(TAPS, dtype=jnp.int32) - HALF
    inband = jnp.abs(offsets)[None, None, :] <= band_width[:, :, None]
    kinds = jnp.arange(KERNELS, dtype=jnp.int32)
    picked = (basis_index[:, None] == kinds[None, :, None, None]) & inband[:, None]
    return jnp.where(picked, psi_value[:, None], jnp.zeros((), BF16))


def local_taps(psi_value, basis_index, band_width, first_row, rows):
    value_pad = jnp.pad(psi_value, ((1, 1), (0, 0), (0, 0)))
    basis_pad = jnp.pad(basis_index, ((1, 1), (0, 0), (0, 0)))
    width_pad = jnp.pad(band_width, ((1, 1), (0, 0)))
    near = coefficients(
        lax.dynamic_slice_in_dim(value_pad, first_row, rows + 2, 0),
        lax.dynamic_slice_in_dim(basis_pad, first_row, rows + 2, 0),
        lax.dynamic_slice_in_dim(width_pad, first_row, rows + 2, 0),
    )
    direct = near[1 : rows + 1]
    adjoint = jnp.stack(
        [near[offset : offset + rows, :, 2 - offset, ::-1] for offset in range(3)], axis=2
    )
    even = parity() == 0
    return jnp.concatenate(
        [jnp.where(even, taps[::-1], taps) for taps in (direct, adjoint)], axis=0
    )


def halves(part, bit):
    size = part.shape[0] // 2
    keep = lax.dynamic_slice_in_dim(part, bit * size, size, 0)
    give = lax.dynamic_slice_in_dim(part, (1 - bit) * size, size, 0)
    return keep, give


def joined(own, other, bit):
    return jnp.where(
        bit == 0, jnp.concatenate([own, other], 0), jnp.concatenate([other, own], 0)
    )


def lat_swap(rows, step):
    return lax.ppermute(rows, "lat", [(i, i ^ step) for i in range(lax.axis_size("lat"))])


def on_device(activations, cotangent, mixing, psi_value, basis_index, band_width):
    channels, rows, columns = activations.shape
    total_rows = lax.axis_size("lat") * rows
    first_row = lax.axis_index("lat") * rows
    half = channels // 2
    far_row = parity()
    field = activations.transpose(1, 2, 0)
    upstream = cotangent.transpose(1, 2, 0)
    to_input = mixing.reshape(KERNELS * channels, channels)

    far_own = lax.dynamic_slice_in_dim(field, far_row, 1, 0)
    far_halo = far_swap(far_own)
    later, far_own = lax.optimization_barrier((field, far_own))
    lon = core_swap(edges_of(later))
    near_own = widened(
        lax.dynamic_slice_in_dim(later, 1 - far_row, 1, 0),
        lax.dynamic_slice_in_dim(lon, 1 - far_row, 1, 0),
    )
    near_halo = near_swap(near_own)
    to_hidden, *tables = banded_tables(
        local_taps(psi_value, basis_index, band_width, first_row, rows), mixing
    )
    far_halo, to_hidden, *tables = lax.optimization_barrier((far_halo, to_hidden, *tables))
    far_edges = core_swap(edges_of(far_halo))
    far_out, far_slope, grad = forward_first(
        field, lon, far_halo, far_edges, tables[1], to_hidden, upstream
    )
    far_slope_halo = far_swap(far_slope[None])
    block_out, near_slope, keep, give = forward_second(
        field, lon, near_halo, tables[0], to_hidden, upstream, far_out, far_slope, grad,
        1.0 / total_rows,
    )
    parts = [core_swap(give[at : at + 304]) for at in range(0, give.shape[0], 304)]
    *parts, far_slope_halo = lax.optimization_barrier((*parts, far_slope_halo))
    got = jnp.concatenate(parts)
    steps = [2**at for at in range((lax.axis_size("lat") - 1).bit_length())]
    mine, give, far_wide, near_wide = first_split(steps[0], keep, got, far_slope, near_slope)
    got = lat_swap(give, steps[0])
    far_slope_edges = core_swap(edges_of(far_slope_halo))
    far_grad = backward_first(
        far_wide, near_wide, far_slope_halo, far_slope_edges, tables[3], to_input, upstream
    )
    got, far_grad, near_wide = lax.optimization_barrier((got, far_grad, near_wide))
    near_slope_halo = near_swap(near_wide)
    for at, step in enumerate(steps[1:-1]):
        mine, give = split(step, mine, got)
        got = lat_swap(give, step)
    own = added(round_kernel, mine, got)
    own = added(total_kernel, own, lat_swap(own, steps[-1]))
    for step in reversed(steps[:-1]):
        own = join(step, own, lat_swap(own, step))
    grad_input = backward_second(
        far_wide, near_wide, near_slope_halo, tables[2], to_input, upstream, far_grad
    )
    own, grad_input = lax.optimization_barrier((own, grad_input))
    grad_mixing = glue(
        final_kernel, jax.ShapeDtypeStruct(mixing.shape, F32), own, core_swap(own), name="final"
    )
    return block_out.transpose(2, 0, 1), grad_input.transpose(2, 0, 1), grad_mixing


def solution(mesh):
    in_specs = (P("member", "lat", "lon"), P("member", "lat", "lon"), P(), P(), P(), P())
    out_specs = (P("member", "lat", "lon"), P("member", "lat", "lon"), P("member", None, None))
    return jax.shard_map(
        on_device, mesh=mesh, in_specs=in_specs, out_specs=out_specs, check_vma=False
    )
```

```python
import math

import jax
import jax.numpy as jnp
from jax import lax
from jax.experimental import pallas as pl
from jax.experimental.pallas import tpu as pltpu
from jax.sharding import PartitionSpec as P

KERNELS = 9
HALF = 16
TAPS = 2 * HALF + 1
BLK = 128
WIN = BLK + 2 * HALF
DEPTH = 512
STEP = 240
SWAP = [(0, 1), (1, 0)]
VMEM = pl.BlockSpec(memory_space=pltpu.VMEM)
BF16, F32 = jnp.bfloat16, jnp.float32


def call(kernel, out_shape, scratch, flops, size, *operands, name, limit):
    return pl.pallas_call(
        kernel,
        out_shape=out_shape,
        in_specs=[VMEM] * len(operands),
        out_specs=jax.tree.map(lambda _: VMEM, out_shape),
        scratch_shapes=scratch,
        compiler_params=pltpu.CompilerParams(vmem_limit_bytes=limit * 2**20),
        cost_estimate=pl.CostEstimate(flops=flops, bytes_accessed=size, transcendentals=0),
        name=name,
    )(*operands)


def tables_kernel(lines_ref, mixing_ref, turned_ref, *out_refs):
    channels = mixing_ref.shape[2]
    for kind in range(KERNELS):
        turned_ref[kind * channels : (kind + 1) * channels] = mixing_ref[kind].T
    for row, out_ref in enumerate(out_refs):
        for kind in range(KERNELS):
            line = jnp.broadcast_to(lines_ref[row, kind : kind + 1, :], (BLK, DEPTH))
            out_ref[kind * BLK : (kind + 1) * BLK, :] = pltpu.roll(
                line, 0, 1, stride=1, stride_axis=0
            ).astype(BF16)


def banded_tables(taps, mixing):
    lead = taps.shape[0]
    kinds, channels, _ = mixing.shape
    lines = jnp.pad(taps.astype(F32), ((0, 0), (0, 0), (0, 0), (0, WIN - TAPS)))
    lines = jnp.pad(lines.reshape(lead, KERNELS, 3 * WIN), ((0, 0), (0, 0), (0, DEPTH - 3 * WIN)))
    turned = jax.ShapeDtypeStruct((kinds * channels, channels), BF16)
    shapes = [turned] + [jax.ShapeDtypeStruct((KERNELS * BLK, DEPTH), BF16)] * lead
    return call(
        tables_kernel, shapes, [], 10**7, 3_000_000, lines, mixing, name="tables", limit=12
    )


def parity():
    return lax.rem(lax.axis_index("lat"), 2)


def place(wide_ref, slot, middle, edges):
    columns = middle.shape[0]
    wide_ref[slot, 0:HALF] = edges[0:HALF]
    wide_ref[slot, HALF : HALF + columns] = middle
    wide_ref[slot, HALF + columns :] = edges[HALF:]


def place_inside(wide_ref, slot, middle_ref, edges_ref):
    lat = lax.axis_index("lat")
    inside = (lat > 0) & (lat < lax.axis_size("lat") - 1)

    @pl.when(inside)
    def _():
        place(wide_ref, slot, middle_ref[0], edges_ref[0])

    @pl.when(jnp.logical_not(inside))
    def _():
        wide_ref[slot] = jnp.zeros(wide_ref.shape[1:], BF16)


def banded_row(table_ref, wide_ref, buffer_ref):
    columns = buffer_ref.shape[0]
    channels = wide_ref.shape[2]
    for block in range(-(-columns // BLK)):
        start = min(block * BLK, columns - BLK)
        window = jnp.concatenate(
            [wide_ref[offset, start : start + WIN] for offset in range(3)], axis=0
        )
        for kind in range(KERNELS):
            out = jnp.dot(
                table_ref[kind * BLK : (kind + 1) * BLK, : 3 * WIN],
                window,
                preferred_element_type=F32,
            )
            buffer_ref[start : start + BLK, kind * channels : (kind + 1) * channels] = (
                out.astype(BF16)
            )


def gelu_parts(hidden):
    cdf = 0.5 * (1.0 + lax.erf(hidden * (1.0 / math.sqrt(2.0))))
    slope = cdf + hidden * jnp.exp(-0.5 * hidden * hidden) * (1.0 / math.sqrt(2.0 * math.pi))
    return hidden * cdf, slope


def gelu_row(field_ref, cot_ref, row, mix_ref, buffer_ref, out_ref, slope_ref, turned_ref):
    columns = buffer_ref.shape[0]
    for start in range(0, columns, STEP):
        part = slice(start, start + STEP)
        hidden = jnp.dot(buffer_ref[part, :], mix_ref[...], preferred_element_type=F32)
        value, derivative = gelu_parts(hidden)
        out_ref[part] = (field_ref[row, part].astype(F32) + value).astype(BF16)
        slope_ref[part] = (cot_ref[row, part].astype(F32) * derivative).astype(BF16)
    turned_ref[...] = slope_ref[...].T


def grad_of(turned_ref, buffer_ref, kind):
    channels = turned_ref.shape[0]
    return jnp.dot(
        turned_ref[...],
        buffer_ref[:, kind * channels : (kind + 1) * channels],
        preferred_element_type=F32,
    )


def first_kernel(
    field_ref, lon_ref, row_ref, edge_ref, table_ref, mix_ref, cot_ref,
    out_ref, slope_ref, buffer_ref, turned_ref, wide_ref,
):
    odd = parity()
    near, far = 1 - odd, odd
    place(wide_ref, 2 - 2 * odd, field_ref[near], lon_ref[near])
    place(wide_ref, 1, field_ref[far], lon_ref[far])
    place_inside(wide_ref, 2 * odd, row_ref, edge_ref)
    banded_row(table_ref, wide_ref, buffer_ref)
    gelu_row(field_ref, cot_ref, far, mix_ref, buffer_ref, out_ref, slope_ref, turned_ref)


def second_kernel(
    scale, field_ref, lon_ref, row_ref, table_ref, mix_ref, cot_ref,
    far_out_ref, far_slope_ref, far_buffer_ref, far_turned_ref,
    out_ref, slope_ref, keep_ref, give_ref, wide_ref, buffer_ref, turned_ref,
):
    odd = parity()
    near, far = 1 - odd, odd
    place(wide_ref, 2 * odd, field_ref[far], lon_ref[far])
    place(wide_ref, 1, field_ref[near], lon_ref[near])
    wide_ref[2 - 2 * odd] = row_ref[0]
    banded_row(table_ref, wide_ref, buffer_ref)
    gelu_row(
        field_ref, cot_ref, near, mix_ref, buffer_ref, out_ref.at[near], slope_ref, turned_ref
    )
    out_ref[far] = far_out_ref[...]
    first = lax.axis_index("lon") == 0
    columns = slope_ref.shape[0]
    channels = turned_ref.shape[0]
    half = channels // 2
    for kind in range(KERNELS):
        grad = scale * (
            grad_of(far_turned_ref, far_buffer_ref, kind)
            + grad_of(turned_ref, buffer_ref, kind)
        )
        low, high = grad[:half], grad[half:]
        part = slice(kind * half, (kind + 1) * half)
        keep_ref[part] = jnp.where(first, low, high)
        give_ref[part] = jnp.where(first, high, low).astype(BF16)
    base = KERNELS * half
    for ref in (far_slope_ref, slope_ref):
        give_ref[base : base + HALF] = ref[columns - HALF :]
        give_ref[base + HALF : base + 2 * HALF] = ref[:HALF]
        base += 2 * HALF


def contract_row(cot_ref, row, mix_ref, buffer_ref, out_ref):
    columns = buffer_ref.shape[0]
    for start in range(0, columns, STEP):
        part = slice(start, start + STEP)
        grad = jnp.dot(buffer_ref[part, :], mix_ref[...], preferred_element_type=F32)
        out_ref[part] = (cot_ref[row, part].astype(F32) + grad).astype(BF16)


def back_first_kernel(
    far_ref, near_ref, row_ref, edge_ref, table_ref, mix_ref, cot_ref,
    out_ref, wide_ref, buffer_ref,
):
    odd = parity()
    wide_ref[2 - 2 * odd] = near_ref[0]
    wide_ref[1] = far_ref[0]
    place_inside(wide_ref, 2 * odd, row_ref, edge_ref)
    banded_row(table_ref, wide_ref, buffer_ref)
    contract_row(cot_ref, odd, mix_ref, buffer_ref, out_ref)


def back_second_kernel(
    far_ref, near_ref, row_ref, table_ref, mix_ref, cot_ref, far_out_ref,
    out_ref, wide_ref, buffer_ref,
):
    odd = parity()
    wide_ref[2 * odd] = far_ref[0]
    wide_ref[1] = near_ref[0]
    wide_ref[2 - 2 * odd] = row_ref[0]
    banded_row(table_ref, wide_ref, buffer_ref)
    contract_row(cot_ref, 1 - odd, mix_ref, buffer_ref, out_ref.at[1 - odd])
    out_ref[odd] = far_out_ref[...]


def lat_bit_clear(step):
    return lax.rem(lax.div(lax.axis_index("lat"), step), 2) == 0


def first_split_kernel(
    step, keep_ref, got_ref, far_ref, near_ref, mine_ref, give_ref, far_wide_ref, near_wide_ref
):
    split_kernel(step, keep_ref, got_ref, mine_ref, give_ref)
    base = keep_ref.shape[0]
    for row_ref, wide_ref in ((far_ref, far_wide_ref), (near_ref, near_wide_ref)):
        columns = row_ref.shape[0]
        wide_ref[0, :HALF] = got_ref[base : base + HALF]
        wide_ref[0, HALF : HALF + columns] = row_ref[...]
        wide_ref[0, HALF + columns :] = got_ref[base + HALF : base + 2 * HALF]
        base += 2 * HALF


def split_kernel(step, keep_ref, got_ref, mine_ref, give_ref):
    half = keep_ref.shape[0] // 2
    clear = lat_bit_clear(step)
    low = keep_ref[:half] + got_ref[:half].astype(F32)
    high = keep_ref[half:] + got_ref[half : 2 * half].astype(F32)
    mine_ref[...] = jnp.where(clear, low, high)
    give_ref[...] = jnp.where(clear, high, low).astype(BF16)


def join_kernel(step, own_ref, got_ref, out_ref):
    half = own_ref.shape[0]
    clear = lat_bit_clear(step)
    out_ref[:half] = jnp.where(clear, own_ref[...], got_ref[...])
    out_ref[half:] = jnp.where(clear, got_ref[...], own_ref[...])


def round_kernel(keep_ref, got_ref, out_ref):
    out_ref[...] = (keep_ref[...] + got_ref[...].astype(F32)).astype(BF16)


def total_kernel(own_ref, got_ref, out_ref):
    out_ref[...] = (own_ref[...].astype(F32) + got_ref[...].astype(F32)).astype(BF16)


def final_kernel(own_ref, got_ref, out_ref):
    kinds, channels, _ = out_ref.shape
    half = channels // 2
    first = lax.axis_index("lon") == 0
    for kind in range(kinds):
        part = slice(kind * half, (kind + 1) * half)
        own, got = own_ref[part].astype(F32), got_ref[part].astype(F32)
        out_ref[kind, :half] = jnp.where(first, own, got)
        out_ref[kind, half:] = jnp.where(first, got, own)


def glue(kernel, shapes, *operands, name):
    return call(kernel, shapes, [], 10**6, 10**6, *operands, name=name, limit=8)


def tiled(rows):
    return rows % 16 == 0


def bit_of(step):
    return (lax.axis_index("lat") // step) % 2


def split(step, keep, got):
    rows, channels = keep.shape
    if not tiled(rows // 2):
        whole = keep + got.astype(F32)
        mine, give = halves(whole, bit_of(step))
        return mine, give.astype(BF16)

    def kernel(*refs):
        split_kernel(step, *refs)

    shapes = (
        jax.ShapeDtypeStruct((rows // 2, channels), F32),
        jax.ShapeDtypeStruct((rows // 2, channels), BF16),
    )
    return glue(kernel, shapes, keep, got, name="split")


def first_split(step, keep, got, far, near):
    rows, channels = keep.shape

    def kernel(*refs):
        first_split_kernel(step, *refs)

    wide = jax.ShapeDtypeStruct((1, far.shape[0] + 2 * HALF, channels), BF16)
    shapes = (
        jax.ShapeDtypeStruct((rows // 2, channels), F32),
        jax.ShapeDtypeStruct((rows // 2, channels), BF16),
        wide,
        wide,
    )
    return glue(kernel, shapes, keep, got, far, near, name="first_split")


def join(step, own, got):
    rows, channels = own.shape
    if not tiled(rows):
        return joined(own, got, bit_of(step))

    def kernel(*refs):
        join_kernel(step, *refs)

    return glue(
        kernel, jax.ShapeDtypeStruct((2 * rows, channels), BF16), own, got, name="join"
    )


def added(kernel, own, got):
    if not tiled(own.shape[0]):
        return (own.astype(F32) + got.astype(F32)).astype(BF16)
    return glue(kernel, jax.ShapeDtypeStruct(own.shape, BF16), own, got, name="added")


def scratch_of(columns, channels):
    return [
        pltpu.VMEM((3, columns + 2 * HALF, channels), BF16),
        pltpu.VMEM((columns, KERNELS * channels), BF16),
    ]


def forward_first(field, lon, row, edge, table, mix, upstream):
    _, columns, channels = field.shape
    shapes = (
        jax.ShapeDtypeStruct((columns, channels), BF16),
        jax.ShapeDtypeStruct((columns, channels), BF16),
        jax.ShapeDtypeStruct((columns, KERNELS * channels), BF16),
        jax.ShapeDtypeStruct((channels, columns), BF16),
    )
    return call(
        first_kernel, shapes, scratch_of(columns, channels)[:1], 25 * 10**8, 4 * 10**6,
        field, lon, row, edge, table, mix, upstream, name="first", limit=16,
    )


def forward_second(field, lon, row, table, mix, upstream, far, scale):
    _, columns, channels = field.shape
    half = KERNELS * channels // 2
    shapes = (
        jax.ShapeDtypeStruct(field.shape, BF16),
        jax.ShapeDtypeStruct((columns, channels), BF16),
        jax.ShapeDtypeStruct((half, channels), F32),
        jax.ShapeDtypeStruct((half + 4 * HALF, channels), BF16),
    )
    turned = pltpu.VMEM((channels, columns), BF16)

    def kernel(*refs):
        second_kernel(scale, *refs)

    return call(
        kernel, shapes, scratch_of(columns, channels) + [turned], 35 * 10**8, 4 * 10**6,
        field, lon, row, table, mix, upstream, *far,
        name="second", limit=16,
    )


def backward_first(far, near, row, edge, table, mix, upstream):
    _, columns, channels = upstream.shape
    return call(
        back_first_kernel, jax.ShapeDtypeStruct((columns, channels), BF16),
        scratch_of(columns, channels), 25 * 10**8, 3 * 10**6,
        far, near, row, edge, table, mix, upstream, name="back_first", limit=10,
    )


def backward_second(far, near, row, table, mix, upstream, far_out):
    _, columns, channels = upstream.shape
    return call(
        back_second_kernel, jax.ShapeDtypeStruct(upstream.shape, BF16),
        scratch_of(columns, channels), 25 * 10**8, 3 * 10**6,
        far, near, row, table, mix, upstream, far_out, name="back_second", limit=10,
    )


def pick_kernel(field_ref, out_ref, sem):
    copy = pltpu.make_async_copy(field_ref.at[pl.ds(parity(), 1)], out_ref, sem)
    copy.start()
    copy.wait()


def pick_far(field):
    _, columns, channels = field.shape
    return pl.pallas_call(
        pick_kernel,
        out_shape=jax.ShapeDtypeStruct((1, columns, channels), BF16),
        in_specs=[pl.BlockSpec(memory_space=pl.ANY)],
        out_specs=VMEM,
        scratch_shapes=[pltpu.SemaphoreType.DMA],
        compiler_params=pltpu.CompilerParams(vmem_limit_bytes=4 * 2**20),
        cost_estimate=pl.CostEstimate(flops=0, bytes_accessed=800_000, transcendentals=0),
        name="pick",
    )(field)


def near_swap(row):
    count = lax.axis_size("lat")
    return lax.ppermute(row, "lat", [(i, i ^ 1) for i in range(count)])


def far_swap(row):
    members, count = lax.axis_size("member"), lax.axis_size("lat")
    pairs = [(i, i + 1) for i in range(1, count - 1, 2)]
    pairs += [(b, a) for a, b in pairs]
    pairs = [(m * count + a, m * count + b) for m in range(members) for a, b in pairs]
    for end in (0, count - 1):
        pairs += [(m * count + end, (m + 1) % members * count + end) for m in range(members)]
    return lax.ppermute(row, ("member", "lat"), pairs)


def edges_of(rows):
    return jnp.concatenate([rows[:, -HALF:], rows[:, :HALF]], axis=1)


def core_swap(rows):
    return lax.ppermute(rows, "lon", SWAP)


def widened(row, edges):
    return jnp.concatenate([edges[:, :HALF], row, edges[:, HALF:]], axis=1)


def local_taps(psi_value, basis_index, band_width, first_row, rows):
    offsets = jnp.arange(TAPS, dtype=jnp.int32) - HALF
    inband = jnp.abs(offsets)[None, None, :] <= band_width[:, :, None]
    value = jnp.where(inband, psi_value.astype(F32), 0.0)
    both = jnp.pad(jnp.stack([value, basis_index.astype(F32)]), ((0, 0), (1, 1), (0, 0), (0, 0)))
    value, kind = lax.dynamic_slice_in_dim(both, first_row, rows + 2, 1)
    kinds = jnp.arange(KERNELS, dtype=jnp.int32).astype(F32)
    near = jnp.where(kind[:, None] == kinds[None, :, None, None], value[:, None], 0.0)
    direct = near[1 : rows + 1]
    adjoint = jnp.stack(
        [near[offset : offset + rows, :, 2 - offset, ::-1] for offset in range(3)], axis=2
    )
    even = parity() == 0
    return jnp.concatenate(
        [jnp.where(even, taps[::-1], taps) for taps in (direct, adjoint)], axis=0
    )


def halves(part, bit):
    size = part.shape[0] // 2
    keep = lax.dynamic_slice_in_dim(part, bit * size, size, 0)
    give = lax.dynamic_slice_in_dim(part, (1 - bit) * size, size, 0)
    return keep, give


def joined(own, other, bit):
    return jnp.where(
        bit == 0, jnp.concatenate([own, other], 0), jnp.concatenate([other, own], 0)
    )


def lat_swap(rows, step):
    return lax.ppermute(rows, "lat", [(i, i ^ step) for i in range(lax.axis_size("lat"))])


def on_device(activations, cotangent, mixing, psi_value, basis_index, band_width):
    channels, rows, columns = activations.shape
    total_rows = lax.axis_size("lat") * rows
    first_row = lax.axis_index("lat") * rows
    half = channels // 2
    far_row = parity()
    field = activations.transpose(1, 2, 0)
    upstream = cotangent.transpose(1, 2, 0)
    to_input = mixing.reshape(KERNELS * channels, channels)

    far_own = pick_far(field)
    far_halo = far_swap(far_own)
    later, far_own = lax.optimization_barrier((field, far_own))
    lon = core_swap(edges_of(later))
    near_own = widened(
        lax.dynamic_slice_in_dim(later, 1 - far_row, 1, 0),
        lax.dynamic_slice_in_dim(lon, 1 - far_row, 1, 0),
    )
    near_halo = near_swap(near_own)
    to_hidden, *tables = banded_tables(
        local_taps(psi_value, basis_index, band_width, first_row, rows), mixing
    )
    far_halo, to_hidden, *tables = lax.optimization_barrier((far_halo, to_hidden, *tables))
    far_edges = core_swap(edges_of(far_halo))
    far = forward_first(
        field, lon, far_halo, far_edges, tables[1], to_hidden, upstream
    )
    far_slope = far[1]
    far_slope_halo = far_swap(far_slope[None])
    block_out, near_slope, keep, give = forward_second(
        field, lon, near_halo, tables[0], to_hidden, upstream, far,
        1.0 / total_rows,
    )
    parts = [core_swap(give[at : at + 304]) for at in range(0, give.shape[0], 304)]
    *parts, far_slope_halo = lax.optimization_barrier((*parts, far_slope_halo))
    got = jnp.concatenate(parts)
    steps = [2**at for at in range((lax.axis_size("lat") - 1).bit_length())]
    mine, give, far_wide, near_wide = first_split(steps[0], keep, got, far_slope, near_slope)
    got = lat_swap(give, steps[0])
    far_slope_edges = core_swap(edges_of(far_slope_halo))
    far_grad = backward_first(
        far_wide, near_wide, far_slope_halo, far_slope_edges, tables[3], to_input, upstream
    )
    got, far_grad, near_wide = lax.optimization_barrier((got, far_grad, near_wide))
    near_slope_halo = near_swap(near_wide)
    for at, step in enumerate(steps[1:-1]):
        mine, give = split(step, mine, got)
        got = lat_swap(give, step)
    own = added(round_kernel, mine, got)
    own = added(total_kernel, own, lat_swap(own, steps[-1]))
    for step in reversed(steps[:-1]):
        own = join(step, own, lat_swap(own, step))
    grad_input = backward_second(
        far_wide, near_wide, near_slope_halo, tables[2], to_input, upstream, far_grad
    )
    own, grad_input = lax.optimization_barrier((own, grad_input))
    grad_mixing = glue(
        final_kernel, jax.ShapeDtypeStruct(mixing.shape, F32), own, core_swap(own), name="final"
    )
    return block_out.transpose(2, 0, 1), grad_input.transpose(2, 0, 1), grad_mixing


def solution(mesh):
    in_specs = (P("member", "lat", "lon"), P("member", "lat", "lon"), P(), P(), P(), P())
    out_specs = (P("member", "lat", "lon"), P("member", "lat", "lon"), P("member", None, None))
    return jax.shard_map(
        on_device, mesh=mesh, in_specs=in_specs, out_specs=out_specs, check_vma=False
    )
```

```python
import math

import jax
import jax.numpy as jnp
from jax import lax
from jax.experimental import pallas as pl
from jax.experimental.pallas import tpu as pltpu
from jax.sharding import PartitionSpec as P

KERNELS = 9
HALF = 16
TAPS = 2 * HALF + 1
BLK = 128
WIN = BLK + 2 * HALF
DEPTH = 512
STEP = 240
SWAP = [(0, 1), (1, 0)]
VMEM = pl.BlockSpec(memory_space=pltpu.VMEM)
BF16, F32 = jnp.bfloat16, jnp.float32


def call(kernel, out_shape, scratch, flops, size, *operands, name, limit):
    return pl.pallas_call(
        kernel,
        out_shape=out_shape,
        in_specs=[VMEM] * len(operands),
        out_specs=jax.tree.map(lambda _: VMEM, out_shape),
        scratch_shapes=scratch,
        compiler_params=pltpu.CompilerParams(vmem_limit_bytes=limit * 2**20),
        cost_estimate=pl.CostEstimate(flops=flops, bytes_accessed=size, transcendentals=0),
        name=name,
    )(*operands)


def tables_kernel(lines_ref, mixing_ref, turned_ref, *out_refs):
    channels = mixing_ref.shape[2]
    for kind in range(KERNELS):
        turned_ref[kind * channels : (kind + 1) * channels] = mixing_ref[kind].T
    for row, out_ref in enumerate(out_refs):
        for kind in range(KERNELS):
            line = jnp.broadcast_to(lines_ref[row, kind : kind + 1, :], (BLK, DEPTH))
            out_ref[kind * BLK : (kind + 1) * BLK, :] = pltpu.roll(
                line, 0, 1, stride=1, stride_axis=0
            ).astype(BF16)


def banded_tables(taps, mixing):
    lead = taps.shape[0]
    kinds, channels, _ = mixing.shape
    lines = jnp.pad(taps.astype(F32), ((0, 0), (0, 0), (0, 0), (0, WIN - TAPS)))
    lines = jnp.pad(lines.reshape(lead, KERNELS, 3 * WIN), ((0, 0), (0, 0), (0, DEPTH - 3 * WIN)))
    turned = jax.ShapeDtypeStruct((kinds * channels, channels), BF16)
    shapes = [turned] + [jax.ShapeDtypeStruct((KERNELS * BLK, DEPTH), BF16)] * lead
    return call(
        tables_kernel, shapes, [], 10**7, 3_000_000, lines, mixing, name="tables", limit=12
    )


def parity():
    return lax.rem(lax.axis_index("lat"), 2)


def place(wide_ref, slot, middle, edges):
    columns = middle.shape[0]
    wide_ref[slot, 0:HALF] = edges[0:HALF]
    wide_ref[slot, HALF : HALF + columns] = middle
    wide_ref[slot, HALF + columns :] = edges[HALF:]


def place_inside(wide_ref, slot, middle_ref, edges_ref):
    lat = lax.axis_index("lat")
    inside = (lat > 0) & (lat < lax.axis_size("lat") - 1)

    @pl.when(inside)
    def _():
        place(wide_ref, slot, middle_ref[0], edges_ref[0])

    @pl.when(jnp.logical_not(inside))
    def _():
        wide_ref[slot] = jnp.zeros(wide_ref.shape[1:], BF16)


def banded_row(table_ref, wide_ref, buffer_ref):
    columns = buffer_ref.shape[0]
    channels = wide_ref.shape[2]
    for block in range(-(-columns // BLK)):
        start = min(block * BLK, columns - BLK)
        window = jnp.concatenate(
            [wide_ref[offset, start : start + WIN] for offset in range(3)], axis=0
        )
        for kind in range(KERNELS):
            out = jnp.dot(
                table_ref[kind * BLK : (kind + 1) * BLK, : 3 * WIN],
                window,
                preferred_element_type=F32,
            )
            buffer_ref[start : start + BLK, kind * channels : (kind + 1) * channels] = (
                out.astype(BF16)
            )


def gelu_parts(hidden):
    cdf = 0.5 * (1.0 + lax.erf(hidden * (1.0 / math.sqrt(2.0))))
    slope = cdf + hidden * jnp.exp(-0.5 * hidden * hidden) * (1.0 / math.sqrt(2.0 * math.pi))
    return hidden * cdf, slope


def gelu_row(field_ref, cot_ref, row, mix_ref, buffer_ref, out_ref, slope_ref, turned_ref):
    columns = buffer_ref.shape[0]
    for start in range(0, columns, STEP):
        part = slice(start, start + STEP)
        hidden = jnp.dot(buffer_ref[part, :], mix_ref[...], preferred_element_type=F32)
        value, derivative = gelu_parts(hidden)
        out_ref[part] = (field_ref[row, part].astype(F32) + value).astype(BF16)
        slope_ref[part] = (cot_ref[row, part].astype(F32) * derivative).astype(BF16)
    turned_ref[...] = slope_ref[...].T


def grad_of(turned_ref, buffer_ref, kind):
    channels = turned_ref.shape[0]
    return jnp.dot(
        turned_ref[...],
        buffer_ref[:, kind * channels : (kind + 1) * channels],
        preferred_element_type=F32,
    )


def first_kernel(
    field_ref, lon_ref, row_ref, edge_ref, table_ref, mix_ref, cot_ref,
    out_ref, slope_ref, buffer_ref, turned_ref, wide_ref,
):
    odd = parity()
    near, far = 1 - odd, odd
    place(wide_ref, 2 - 2 * odd, field_ref[near], lon_ref[near])
    place(wide_ref, 1, field_ref[far], lon_ref[far])
    place_inside(wide_ref, 2 * odd, row_ref, edge_ref)
    banded_row(table_ref, wide_ref, buffer_ref)
    gelu_row(field_ref, cot_ref, far, mix_ref, buffer_ref, out_ref, slope_ref, turned_ref)


def second_kernel(
    scale, field_ref, lon_ref, row_ref, table_ref, mix_ref, cot_ref,
    far_out_ref, far_slope_ref, far_buffer_ref, far_turned_ref,
    out_ref, slope_ref, keep_ref, give_ref, wide_ref, buffer_ref, turned_ref,
):
    odd = parity()
    near, far = 1 - odd, odd
    place(wide_ref, 2 * odd, field_ref[far], lon_ref[far])
    place(wide_ref, 1, field_ref[near], lon_ref[near])
    wide_ref[2 - 2 * odd] = row_ref[0]
    banded_row(table_ref, wide_ref, buffer_ref)
    gelu_row(
        field_ref, cot_ref, near, mix_ref, buffer_ref, out_ref.at[near], slope_ref, turned_ref
    )
    out_ref[far] = far_out_ref[...]
    first = lax.axis_index("lon") == 0
    columns = slope_ref.shape[0]
    channels = turned_ref.shape[0]
    half = channels // 2
    for kind in range(KERNELS):
        grad = scale * (
            grad_of(far_turned_ref, far_buffer_ref, kind)
            + grad_of(turned_ref, buffer_ref, kind)
        )
        low, high = grad[:half], grad[half:]
        part = slice(kind * half, (kind + 1) * half)
        keep_ref[part] = jnp.where(first, low, high)
        give_ref[part] = jnp.where(first, high, low).astype(BF16)
    base = KERNELS * half
    for ref in (far_slope_ref, slope_ref):
        give_ref[base : base + HALF] = ref[columns - HALF :]
        give_ref[base + HALF : base + 2 * HALF] = ref[:HALF]
        base += 2 * HALF


def contract_row(cot_ref, row, mix_ref, buffer_ref, out_ref):
    columns = buffer_ref.shape[0]
    for start in range(0, columns, STEP):
        part = slice(start, start + STEP)
        grad = jnp.dot(buffer_ref[part, :], mix_ref[...], preferred_element_type=F32)
        out_ref[part] = (cot_ref[row, part].astype(F32) + grad).astype(BF16)


def back_first_kernel(
    far_ref, near_ref, row_ref, edge_ref, table_ref, mix_ref, cot_ref,
    out_ref, wide_ref, buffer_ref,
):
    odd = parity()
    wide_ref[2 - 2 * odd] = near_ref[0]
    wide_ref[1] = far_ref[0]
    place_inside(wide_ref, 2 * odd, row_ref, edge_ref)
    banded_row(table_ref, wide_ref, buffer_ref)
    contract_row(cot_ref, odd, mix_ref, buffer_ref, out_ref)


def back_second_kernel(
    far_ref, near_ref, row_ref, table_ref, mix_ref, cot_ref, far_out_ref,
    out_ref, wide_ref, buffer_ref,
):
    odd = parity()
    wide_ref[2 * odd] = far_ref[0]
    wide_ref[1] = near_ref[0]
    wide_ref[2 - 2 * odd] = row_ref[0]
    banded_row(table_ref, wide_ref, buffer_ref)
    contract_row(cot_ref, 1 - odd, mix_ref, buffer_ref, out_ref.at[1 - odd])
    out_ref[odd] = far_out_ref[...]


def lat_bit_clear(step):
    return lax.rem(lax.div(lax.axis_index("lat"), step), 2) == 0


def first_split_kernel(
    steps, keep_ref, got_ref, far_ref, near_ref,
    low_mine_ref, low_give_ref, high_mine_ref, high_give_ref, far_wide_ref, near_wide_ref,
):
    base = keep_ref.shape[0]
    half = base // 2
    split_kernel(
        steps[0], keep_ref.at[pl.ds(0, half)], got_ref.at[pl.ds(0, half)], low_mine_ref, low_give_ref
    )
    split_kernel(
        steps[1], keep_ref.at[pl.ds(half, half)], got_ref.at[pl.ds(half, half)], high_mine_ref, high_give_ref
    )
    for row_ref, wide_ref in ((far_ref, far_wide_ref), (near_ref, near_wide_ref)):
        columns = row_ref.shape[0]
        wide_ref[0, :HALF] = got_ref[base : base + HALF]
        wide_ref[0, HALF : HALF + columns] = row_ref[...]
        wide_ref[0, HALF + columns :] = got_ref[base + HALF : base + 2 * HALF]
        base += 2 * HALF


def split_kernel(step, keep_ref, got_ref, mine_ref, give_ref):
    half = keep_ref.shape[0] // 2
    clear = lat_bit_clear(step)
    low = keep_ref[:half] + got_ref[:half].astype(F32)
    high = keep_ref[half:] + got_ref[half : 2 * half].astype(F32)
    mine_ref[...] = jnp.where(clear, low, high)
    give_ref[...] = jnp.where(clear, high, low).astype(BF16)


def join_kernel(step, own_ref, got_ref, out_ref):
    half = own_ref.shape[0]
    clear = lat_bit_clear(step)
    out_ref[:half] = jnp.where(clear, own_ref[...], got_ref[...])
    out_ref[half:] = jnp.where(clear, got_ref[...], own_ref[...])


def round_kernel(keep_ref, got_ref, out_ref):
    out_ref[...] = (keep_ref[...] + got_ref[...].astype(F32)).astype(BF16)


def total_kernel(own_ref, got_ref, out_ref):
    out_ref[...] = (own_ref[...].astype(F32) + got_ref[...].astype(F32)).astype(BF16)


def final_kernel(own_ref, got_ref, out_ref):
    kinds, channels, _ = out_ref.shape
    half = channels // 2
    first = lax.axis_index("lon") == 0
    for kind in range(kinds):
        part = slice(kind * half, (kind + 1) * half)
        own, got = own_ref[part].astype(F32), got_ref[part].astype(F32)
        out_ref[kind, :half] = jnp.where(first, own, got)
        out_ref[kind, half:] = jnp.where(first, got, own)


def glue(kernel, shapes, *operands, name):
    return call(kernel, shapes, [], 10**6, 10**6, *operands, name=name, limit=8)


def tiled(rows):
    return rows % 16 == 0


def bit_of(step):
    return (lax.axis_index("lat") // step) % 2


def split(step, keep, got):
    rows, channels = keep.shape
    if not tiled(rows // 2):
        whole = keep + got.astype(F32)
        mine, give = halves(whole, bit_of(step))
        return mine, give.astype(BF16)

    def kernel(*refs):
        split_kernel(step, *refs)

    shapes = (
        jax.ShapeDtypeStruct((rows // 2, channels), F32),
        jax.ShapeDtypeStruct((rows // 2, channels), BF16),
    )
    return glue(kernel, shapes, keep, got, name="split")


def first_split(steps, keep, got, far, near):
    rows, channels = keep.shape

    def kernel(*refs):
        first_split_kernel(steps, *refs)

    wide = jax.ShapeDtypeStruct((1, far.shape[0] + 2 * HALF, channels), BF16)
    mine = jax.ShapeDtypeStruct((rows // 4, channels), F32)
    give = jax.ShapeDtypeStruct((rows // 4, channels), BF16)
    shapes = (mine, give, mine, give, wide, wide)
    return glue(kernel, shapes, keep, got, far, near, name="first_split")


def join(step, own, got):
    rows, channels = own.shape
    if not tiled(rows):
        return joined(own, got, bit_of(step))

    def kernel(*refs):
        join_kernel(step, *refs)

    return glue(
        kernel, jax.ShapeDtypeStruct((2 * rows, channels), BF16), own, got, name="join"
    )


def added(kernel, own, got):
    if not tiled(own.shape[0]):
        return (own.astype(F32) + got.astype(F32)).astype(BF16)
    return glue(kernel, jax.ShapeDtypeStruct(own.shape, BF16), own, got, name="added")


def scratch_of(columns, channels):
    return [
        pltpu.VMEM((3, columns + 2 * HALF, channels), BF16),
        pltpu.VMEM((columns, KERNELS * channels), BF16),
    ]


def forward_first(field, lon, row, edge, table, mix, upstream):
    _, columns, channels = field.shape
    shapes = (
        jax.ShapeDtypeStruct((columns, channels), BF16),
        jax.ShapeDtypeStruct((columns, channels), BF16),
        jax.ShapeDtypeStruct((columns, KERNELS * channels), BF16),
        jax.ShapeDtypeStruct((channels, columns), BF16),
    )
    return call(
        first_kernel, shapes, scratch_of(columns, channels)[:1], 25 * 10**8, 4 * 10**6,
        field, lon, row, edge, table, mix, upstream, name="first", limit=16,
    )


def forward_second(field, lon, row, table, mix, upstream, far, scale):
    _, columns, channels = field.shape
    half = KERNELS * channels // 2
    shapes = (
        jax.ShapeDtypeStruct(field.shape, BF16),
        jax.ShapeDtypeStruct((columns, channels), BF16),
        jax.ShapeDtypeStruct((half, channels), F32),
        jax.ShapeDtypeStruct((half + 4 * HALF, channels), BF16),
    )
    turned = pltpu.VMEM((channels, columns), BF16)

    def kernel(*refs):
        second_kernel(scale, *refs)

    return call(
        kernel, shapes, scratch_of(columns, channels) + [turned], 35 * 10**8, 4 * 10**6,
        field, lon, row, table, mix, upstream, *far,
        name="second", limit=16,
    )


def backward_first(far, near, row, edge, table, mix, upstream):
    _, columns, channels = upstream.shape
    return call(
        back_first_kernel, jax.ShapeDtypeStruct((columns, channels), BF16),
        scratch_of(columns, channels), 25 * 10**8, 3 * 10**6,
        far, near, row, edge, table, mix, upstream, name="back_first", limit=10,
    )


def backward_second(far, near, row, table, mix, upstream, far_out):
    _, columns, channels = upstream.shape
    return call(
        back_second_kernel, jax.ShapeDtypeStruct(upstream.shape, BF16),
        scratch_of(columns, channels), 25 * 10**8, 3 * 10**6,
        far, near, row, table, mix, upstream, far_out, name="back_second", limit=10,
    )


def pick_kernel(field_ref, out_ref, sem):
    copy = pltpu.make_async_copy(field_ref.at[pl.ds(parity(), 1)], out_ref, sem)
    copy.start()
    copy.wait()


def pick_far(field):
    _, columns, channels = field.shape
    return pl.pallas_call(
        pick_kernel,
        out_shape=jax.ShapeDtypeStruct((1, columns, channels), BF16),
        in_specs=[pl.BlockSpec(memory_space=pl.ANY)],
        out_specs=VMEM,
        scratch_shapes=[pltpu.SemaphoreType.DMA],
        compiler_params=pltpu.CompilerParams(vmem_limit_bytes=4 * 2**20),
        cost_estimate=pl.CostEstimate(flops=0, bytes_accessed=800_000, transcendentals=0),
        name="pick",
    )(field)


def near_swap(row):
    count = lax.axis_size("lat")
    return lax.ppermute(row, "lat", [(i, i ^ 1) for i in range(count)])


def far_swap(row):
    members, count = lax.axis_size("member"), lax.axis_size("lat")
    pairs = [(i, i + 1) for i in range(1, count - 1, 2)]
    pairs += [(b, a) for a, b in pairs]
    pairs = [(m * count + a, m * count + b) for m in range(members) for a, b in pairs]
    for end in (0, count - 1):
        pairs += [(m * count + end, (m + 1) % members * count + end) for m in range(members)]
    return lax.ppermute(row, ("member", "lat"), pairs)


def edges_of(rows):
    return jnp.concatenate([rows[:, -HALF:], rows[:, :HALF]], axis=1)


def core_swap(rows):
    return lax.ppermute(rows, "lon", SWAP)


def widened(row, edges):
    return jnp.concatenate([edges[:, :HALF], row, edges[:, HALF:]], axis=1)


def local_taps(psi_value, basis_index, band_width, first_row, rows):
    offsets = jnp.arange(TAPS, dtype=jnp.int32) - HALF
    inband = jnp.abs(offsets)[None, None, :] <= band_width[:, :, None]
    value = jnp.where(inband, psi_value.astype(F32), 0.0)
    both = jnp.pad(jnp.stack([value, basis_index.astype(F32)]), ((0, 0), (1, 1), (0, 0), (0, 0)))
    value, kind = lax.dynamic_slice_in_dim(both, first_row, rows + 2, 1)
    kinds = jnp.arange(KERNELS, dtype=jnp.int32).astype(F32)
    near = jnp.where(kind[:, None] == kinds[None, :, None, None], value[:, None], 0.0)
    direct = near[1 : rows + 1]
    adjoint = jnp.stack(
        [near[offset : offset + rows, :, 2 - offset, ::-1] for offset in range(3)], axis=2
    )
    even = parity() == 0
    return jnp.concatenate(
        [jnp.where(even, taps[::-1], taps) for taps in (direct, adjoint)], axis=0
    )


def halves(part, bit):
    size = part.shape[0] // 2
    keep = lax.dynamic_slice_in_dim(part, bit * size, size, 0)
    give = lax.dynamic_slice_in_dim(part, (1 - bit) * size, size, 0)
    return keep, give


def joined(own, other, bit):
    return jnp.where(
        bit == 0, jnp.concatenate([own, other], 0), jnp.concatenate([other, own], 0)
    )


def lat_swap(rows, step):
    return lax.ppermute(rows, "lat", [(i, i ^ step) for i in range(lax.axis_size("lat"))])


def on_device(activations, cotangent, mixing, psi_value, basis_index, band_width):
    channels, rows, columns = activations.shape
    total_rows = lax.axis_size("lat") * rows
    first_row = lax.axis_index("lat") * rows
    half = channels // 2
    far_row = parity()
    field = activations.transpose(1, 2, 0)
    upstream = cotangent.transpose(1, 2, 0)
    to_input = mixing.reshape(KERNELS * channels, channels)

    far_own = pick_far(field)
    far_halo = far_swap(far_own)
    later, far_own = lax.optimization_barrier((field, far_own))
    lon = core_swap(edges_of(later))
    near_own = widened(
        lax.dynamic_slice_in_dim(later, 1 - far_row, 1, 0),
        lax.dynamic_slice_in_dim(lon, 1 - far_row, 1, 0),
    )
    near_halo = near_swap(near_own)
    to_hidden, *tables = banded_tables(
        local_taps(psi_value, basis_index, band_width, first_row, rows), mixing
    )
    far_halo, to_hidden, *tables = lax.optimization_barrier((far_halo, to_hidden, *tables))
    far_edges = core_swap(edges_of(far_halo))
    far = forward_first(
        field, lon, far_halo, far_edges, tables[1], to_hidden, upstream
    )
    far_slope = far[1]
    far_slope_halo = far_swap(far_slope[None])
    block_out, near_slope, keep, give = forward_second(
        field, lon, near_halo, tables[0], to_hidden, upstream, far,
        1.0 / total_rows,
    )
    parts = [core_swap(give[at : at + 304]) for at in range(0, give.shape[0], 304)]
    *parts, far_slope_halo = lax.optimization_barrier((*parts, far_slope_halo))
    got = jnp.concatenate(parts)
    steps = [2**at for at in range((lax.axis_size("lat") - 1).bit_length())]
    low, low_give, high, high_give, far_wide, near_wide = first_split(
        steps[:2], keep, got, far_slope, near_slope
    )
    low_got, high_got = lat_swap(low_give, steps[0]), lat_swap(high_give, steps[1])
    far_slope_edges = core_swap(edges_of(far_slope_halo))
    far_grad = backward_first(
        far_wide, near_wide, far_slope_halo, far_slope_edges, tables[3], to_input, upstream
    )
    low_got, high_got, far_grad = lax.optimization_barrier((low_got, high_got, far_grad))
    low, low_give = split(steps[1], low, low_got)
    high, high_give = split(steps[0], high, high_got)
    low_got, high_got = lat_swap(low_give, steps[1]), lat_swap(high_give, steps[0])
    high_got, near_wide = lax.optimization_barrier((high_got, near_wide))
    near_slope_halo = near_swap(near_wide)
    mine = jnp.concatenate([low, high])
    got = jnp.concatenate([low_got, high_got])
    for step in steps[2:-1]:
        mine, give = split(step, mine, got)
        got = lat_swap(give, step)
    own = added(round_kernel, mine, got)
    own = added(total_kernel, own, lat_swap(own, steps[-1]))
    for step in reversed(steps[2:-1]):
        own = join(step, own, lat_swap(own, step))
    low, high = jnp.split(own, 2)
    low_got, high_got = lat_swap(low, steps[1]), lat_swap(high, steps[0])
    low, high = join(steps[1], low, low_got), join(steps[0], high, high_got)
    low, high, near_slope_halo = lax.optimization_barrier((low, high, near_slope_halo))
    low_got, high_got = lat_swap(low, steps[0]), lat_swap(high, steps[1])
    grad_input = backward_second(
        far_wide, near_wide, near_slope_halo, tables[2], to_input, upstream, far_grad
    )
    low_got, high_got, grad_input = lax.optimization_barrier((low_got, high_got, grad_input))
    own = jnp.concatenate([join(steps[0], low, low_got), join(steps[1], high, high_got)])
    grad_mixing = glue(
        final_kernel, jax.ShapeDtypeStruct(mixing.shape, F32), own, core_swap(own), name="final"
    )
    return block_out.transpose(2, 0, 1), grad_input.transpose(2, 0, 1), grad_mixing


def solution(mesh):
    in_specs = (P("member", "lat", "lon"), P("member", "lat", "lon"), P(), P(), P(), P())
    out_specs = (P("member", "lat", "lon"), P("member", "lat", "lon"), P("member", None, None))
    return jax.shard_map(
        on_device, mesh=mesh, in_specs=in_specs, out_specs=out_specs, check_vma=False
    )
```

```python
import math

import jax
import jax.numpy as jnp
from jax import lax
from jax.experimental import pallas as pl
from jax.experimental.pallas import tpu as pltpu
from jax.sharding import PartitionSpec as P

KERNELS = 9
HALF = 16
TAPS = 2 * HALF + 1
BLK = 128
WIN = BLK + 2 * HALF
DEPTH = 512
STEP = 240
SWAP = [(0, 1), (1, 0)]
VMEM = pl.BlockSpec(memory_space=pltpu.VMEM)
BF16, F32 = jnp.bfloat16, jnp.float32


def call(kernel, out_shape, scratch, flops, size, *operands, name, limit):
    return pl.pallas_call(
        kernel,
        out_shape=out_shape,
        in_specs=[VMEM] * len(operands),
        out_specs=jax.tree.map(lambda _: VMEM, out_shape),
        scratch_shapes=scratch,
        compiler_params=pltpu.CompilerParams(vmem_limit_bytes=limit * 2**20),
        cost_estimate=pl.CostEstimate(flops=flops, bytes_accessed=size, transcendentals=0),
        name=name,
    )(*operands)


def tables_kernel(lines_ref, mixing_ref, turned_ref, *out_refs):
    channels = mixing_ref.shape[2]
    for kind in range(KERNELS):
        turned_ref[kind * channels : (kind + 1) * channels] = mixing_ref[kind].T
    for row, out_ref in enumerate(out_refs):
        for kind in range(KERNELS):
            line = jnp.broadcast_to(lines_ref[row, kind : kind + 1, :], (BLK, DEPTH))
            out_ref[kind * BLK : (kind + 1) * BLK, :] = pltpu.roll(
                line, 0, 1, stride=1, stride_axis=0
            ).astype(BF16)


def banded_tables(taps, mixing):
    lead = taps.shape[0]
    kinds, channels, _ = mixing.shape
    lines = jnp.pad(taps.astype(F32), ((0, 0), (0, 0), (0, 0), (0, WIN - TAPS)))
    lines = jnp.pad(lines.reshape(lead, KERNELS, 3 * WIN), ((0, 0), (0, 0), (0, DEPTH - 3 * WIN)))
    turned = jax.ShapeDtypeStruct((kinds * channels, channels), BF16)
    shapes = [turned] + [jax.ShapeDtypeStruct((KERNELS * BLK, DEPTH), BF16)] * lead
    return call(
        tables_kernel, shapes, [], 10**7, 3_000_000, lines, mixing, name="tables", limit=12
    )


def parity():
    return lax.rem(lax.axis_index("lat"), 2)


def place(wide_ref, slot, middle, edges):
    columns = middle.shape[0]
    wide_ref[slot, 0:HALF] = edges[0:HALF]
    wide_ref[slot, HALF : HALF + columns] = middle
    wide_ref[slot, HALF + columns :] = edges[HALF:]


def place_inside(wide_ref, slot, middle_ref, edges_ref):
    lat = lax.axis_index("lat")
    inside = (lat > 0) & (lat < lax.axis_size("lat") - 1)

    @pl.when(inside)
    def _():
        place(wide_ref, slot, middle_ref[0], edges_ref[0])

    @pl.when(jnp.logical_not(inside))
    def _():
        wide_ref[slot] = jnp.zeros(wide_ref.shape[1:], BF16)


def banded_row(table_ref, wide_ref, buffer_ref):
    columns = buffer_ref.shape[0]
    channels = wide_ref.shape[2]
    for block in range(-(-columns // BLK)):
        start = min(block * BLK, columns - BLK)
        window = jnp.concatenate(
            [wide_ref[offset, start : start + WIN] for offset in range(3)], axis=0
        )
        for kind in range(KERNELS):
            out = jnp.dot(
                table_ref[kind * BLK : (kind + 1) * BLK, : 3 * WIN],
                window,
                preferred_element_type=F32,
            )
            buffer_ref[start : start + BLK, kind * channels : (kind + 1) * channels] = (
                out.astype(BF16)
            )


def gelu_parts(hidden):
    cdf = 0.5 * (1.0 + lax.erf(hidden * (1.0 / math.sqrt(2.0))))
    slope = cdf + hidden * jnp.exp(-0.5 * hidden * hidden) * (1.0 / math.sqrt(2.0 * math.pi))
    return hidden * cdf, slope


def gelu_row(field_ref, cot_ref, row, mix_ref, buffer_ref, out_ref, slope_ref, turned_ref):
    columns = buffer_ref.shape[0]
    for start in range(0, columns, STEP):
        part = slice(start, start + STEP)
        hidden = jnp.dot(buffer_ref[part, :], mix_ref[...], preferred_element_type=F32)
        value, derivative = gelu_parts(hidden)
        out_ref[part] = (field_ref[row, part].astype(F32) + value).astype(BF16)
        slope_ref[part] = (cot_ref[row, part].astype(F32) * derivative).astype(BF16)
    turned_ref[...] = slope_ref[...].T


def grad_of(turned_ref, buffer_ref, kind):
    channels = turned_ref.shape[0]
    return jnp.dot(
        turned_ref[...],
        buffer_ref[:, kind * channels : (kind + 1) * channels],
        preferred_element_type=F32,
    )


def first_kernel(
    field_ref, lon_ref, row_ref, edge_ref, table_ref, mix_ref, cot_ref,
    out_ref, slope_ref, buffer_ref, turned_ref, wide_ref,
):
    odd = parity()
    near, far = 1 - odd, odd
    place(wide_ref, 2 - 2 * odd, field_ref[near], lon_ref[near])
    place(wide_ref, 1, field_ref[far], lon_ref[far])
    place_inside(wide_ref, 2 * odd, row_ref, edge_ref)
    banded_row(table_ref, wide_ref, buffer_ref)
    gelu_row(field_ref, cot_ref, far, mix_ref, buffer_ref, out_ref, slope_ref, turned_ref)


def second_kernel(
    scale, field_ref, lon_ref, row_ref, table_ref, mix_ref, cot_ref,
    far_out_ref, far_slope_ref, far_buffer_ref, far_turned_ref,
    out_ref, slope_ref, keep_ref, give_ref, wide_ref, buffer_ref, turned_ref,
):
    odd = parity()
    near, far = 1 - odd, odd
    place(wide_ref, 2 * odd, field_ref[far], lon_ref[far])
    place(wide_ref, 1, field_ref[near], lon_ref[near])
    wide_ref[2 - 2 * odd] = row_ref[0]
    banded_row(table_ref, wide_ref, buffer_ref)
    gelu_row(
        field_ref, cot_ref, near, mix_ref, buffer_ref, out_ref.at[near], slope_ref, turned_ref
    )
    out_ref[far] = far_out_ref[...]
    first = lax.axis_index("lon") == 0
    columns = slope_ref.shape[0]
    channels = turned_ref.shape[0]
    half = channels // 2
    for kind in range(KERNELS):
        grad = scale * (
            grad_of(far_turned_ref, far_buffer_ref, kind)
            + grad_of(turned_ref, buffer_ref, kind)
        )
        low, high = grad[:half], grad[half:]
        part = slice(kind * half, (kind + 1) * half)
        keep_ref[part] = jnp.where(first, low, high)
        give_ref[part] = jnp.where(first, high, low).astype(BF16)
    base = KERNELS * half
    for ref in (far_slope_ref, slope_ref):
        give_ref[base : base + HALF] = ref[columns - HALF :]
        give_ref[base + HALF : base + 2 * HALF] = ref[:HALF]
        base += 2 * HALF


def contract_row(cot_ref, row, mix_ref, buffer_ref, out_ref):
    columns = buffer_ref.shape[0]
    for start in range(0, columns, STEP):
        part = slice(start, start + STEP)
        grad = jnp.dot(buffer_ref[part, :], mix_ref[...], preferred_element_type=F32)
        out_ref[part] = (cot_ref[row, part].astype(F32) + grad).astype(BF16)


def back_first_kernel(
    far_ref, near_ref, row_ref, edge_ref, table_ref, mix_ref, cot_ref,
    out_ref, wide_ref, buffer_ref,
):
    odd = parity()
    wide_ref[2 - 2 * odd] = near_ref[0]
    wide_ref[1] = far_ref[0]
    place_inside(wide_ref, 2 * odd, row_ref, edge_ref)
    banded_row(table_ref, wide_ref, buffer_ref)
    contract_row(cot_ref, odd, mix_ref, buffer_ref, out_ref)


def back_second_kernel(
    far_ref, near_ref, row_ref, table_ref, mix_ref, cot_ref, far_out_ref,
    out_ref, wide_ref, buffer_ref,
):
    odd = parity()
    wide_ref[2 * odd] = far_ref[0]
    wide_ref[1] = near_ref[0]
    wide_ref[2 - 2 * odd] = row_ref[0]
    banded_row(table_ref, wide_ref, buffer_ref)
    contract_row(cot_ref, 1 - odd, mix_ref, buffer_ref, out_ref.at[1 - odd])
    out_ref[odd] = far_out_ref[...]


def lat_bit_clear(step):
    return lax.rem(lax.div(lax.axis_index("lat"), step), 2) == 0


def first_split_kernel(
    steps, keep_ref, got_ref, far_ref, near_ref,
    low_mine_ref, low_give_ref, high_mine_ref, high_give_ref, far_wide_ref, near_wide_ref,
):
    base = keep_ref.shape[0]
    half = base // 2
    split_kernel(
        steps[0], keep_ref.at[pl.ds(0, half)], got_ref.at[pl.ds(0, half)], low_mine_ref, low_give_ref
    )
    split_kernel(
        steps[1], keep_ref.at[pl.ds(half, half)], got_ref.at[pl.ds(half, half)], high_mine_ref, high_give_ref
    )
    for row_ref, wide_ref in ((far_ref, far_wide_ref), (near_ref, near_wide_ref)):
        columns = row_ref.shape[0]
        wide_ref[0, :HALF] = got_ref[base : base + HALF]
        wide_ref[0, HALF : HALF + columns] = row_ref[...]
        wide_ref[0, HALF + columns :] = got_ref[base + HALF : base + 2 * HALF]
        base += 2 * HALF


def split_kernel(step, keep_ref, got_ref, mine_ref, give_ref):
    half = keep_ref.shape[0] // 2
    clear = lat_bit_clear(step)
    low = keep_ref[:half] + got_ref[:half].astype(F32)
    high = keep_ref[half:] + got_ref[half : 2 * half].astype(F32)
    mine_ref[...] = jnp.where(clear, low, high)
    give_ref[...] = jnp.where(clear, high, low).astype(BF16)


def join_kernel(step, own_ref, got_ref, out_ref):
    half = own_ref.shape[0]
    clear = lat_bit_clear(step)
    out_ref[:half] = jnp.where(clear, own_ref[...], got_ref[...])
    out_ref[half:] = jnp.where(clear, got_ref[...], own_ref[...])


def round_kernel(keep_ref, got_ref, out_ref):
    out_ref[...] = (keep_ref[...] + got_ref[...].astype(F32)).astype(BF16)


def total_kernel(own_ref, got_ref, out_ref):
    out_ref[...] = (own_ref[...].astype(F32) + got_ref[...].astype(F32)).astype(BF16)


def place_kernel(parts, column_of, *refs):
    given = refs[: len(parts)]
    out_ref, stage_ref, sems = refs[-3:]
    half = out_ref.shape[1] // 2
    column = lax.axis_index("lon")
    if column_of == "other":
        column = 1 - column
    copies = []
    at = 0
    for base, ref in zip(parts, given):
        row, end = base, base + ref.shape[0]
        while row < end:
            count = min(half - row % half, end - row)
            stage_ref[at : at + count] = ref[row - base : row - base + count].astype(F32)
            start = pl.multiple_of(row % half + column * half, 64)
            copy = pltpu.make_async_copy(
                stage_ref.at[pl.ds(at, count)],
                out_ref.at[row // half, pl.ds(start, count)],
                sems.at[len(copies)],
            )
            copy.start()
            copies.append(copy)
            row, at = row + count, at + count
    for copy in copies:
        copy.wait()


def placed(shape, parts, given, column_of, *before):
    rows, channels = sum(part.shape[0] for part in given), shape[2]

    def kernel(*refs):
        place_kernel(parts, column_of, *refs)

    anywhere = pl.BlockSpec(memory_space=pl.ANY)
    return pl.pallas_call(
        kernel,
        out_shape=jax.ShapeDtypeStruct(shape, F32),
        in_specs=[VMEM] * len(given) + [anywhere] * len(before),
        out_specs=anywhere,
        scratch_shapes=[pltpu.VMEM((rows, channels), F32), pltpu.SemaphoreType.DMA((16,))],
        input_output_aliases={len(given): 0} if before else {},
        compiler_params=pltpu.CompilerParams(vmem_limit_bytes=8 * 2**20),
        cost_estimate=pl.CostEstimate(flops=0, bytes_accessed=10**6, transcendentals=0),
        name="placed",
    )(*given, *before)


def glue(kernel, shapes, *operands, name):
    return call(kernel, shapes, [], 10**6, 10**6, *operands, name=name, limit=8)


def tiled(rows):
    return rows % 16 == 0


def bit_of(step):
    return (lax.axis_index("lat") // step) % 2


def split(step, keep, got):
    rows, channels = keep.shape
    if not tiled(rows // 2):
        whole = keep + got.astype(F32)
        mine, give = halves(whole, bit_of(step))
        return mine, give.astype(BF16)

    def kernel(*refs):
        split_kernel(step, *refs)

    shapes = (
        jax.ShapeDtypeStruct((rows // 2, channels), F32),
        jax.ShapeDtypeStruct((rows // 2, channels), BF16),
    )
    return glue(kernel, shapes, keep, got, name="split")


def first_split(steps, keep, got, far, near):
    rows, channels = keep.shape

    def kernel(*refs):
        first_split_kernel(steps, *refs)

    wide = jax.ShapeDtypeStruct((1, far.shape[0] + 2 * HALF, channels), BF16)
    mine = jax.ShapeDtypeStruct((rows // 4, channels), F32)
    give = jax.ShapeDtypeStruct((rows // 4, channels), BF16)
    shapes = (mine, give, mine, give, wide, wide)
    return glue(kernel, shapes, keep, got, far, near, name="first_split")


def join(step, own, got):
    rows, channels = own.shape
    if not tiled(rows):
        return joined(own, got, bit_of(step))

    def kernel(*refs):
        join_kernel(step, *refs)

    return glue(
        kernel, jax.ShapeDtypeStruct((2 * rows, channels), BF16), own, got, name="join"
    )


def added(kernel, own, got):
    if not tiled(own.shape[0]):
        return (own.astype(F32) + got.astype(F32)).astype(BF16)
    return glue(kernel, jax.ShapeDtypeStruct(own.shape, BF16), own, got, name="added")


def scratch_of(columns, channels):
    return [
        pltpu.VMEM((3, columns + 2 * HALF, channels), BF16),
        pltpu.VMEM((columns, KERNELS * channels), BF16),
    ]


def forward_first(field, lon, row, edge, table, mix, upstream):
    _, columns, channels = field.shape
    shapes = (
        jax.ShapeDtypeStruct((columns, channels), BF16),
        jax.ShapeDtypeStruct((columns, channels), BF16),
        jax.ShapeDtypeStruct((columns, KERNELS * channels), BF16),
        jax.ShapeDtypeStruct((channels, columns), BF16),
    )
    return call(
        first_kernel, shapes, scratch_of(columns, channels)[:1], 25 * 10**8, 4 * 10**6,
        field, lon, row, edge, table, mix, upstream, name="first", limit=16,
    )


def forward_second(field, lon, row, table, mix, upstream, far, scale):
    _, columns, channels = field.shape
    half = KERNELS * channels // 2
    shapes = (
        jax.ShapeDtypeStruct(field.shape, BF16),
        jax.ShapeDtypeStruct((columns, channels), BF16),
        jax.ShapeDtypeStruct((half, channels), F32),
        jax.ShapeDtypeStruct((half + 4 * HALF, channels), BF16),
    )
    turned = pltpu.VMEM((channels, columns), BF16)

    def kernel(*refs):
        second_kernel(scale, *refs)

    return call(
        kernel, shapes, scratch_of(columns, channels) + [turned], 35 * 10**8, 4 * 10**6,
        field, lon, row, table, mix, upstream, *far,
        name="second", limit=16,
    )


def backward_first(far, near, row, edge, table, mix, upstream):
    _, columns, channels = upstream.shape
    return call(
        back_first_kernel, jax.ShapeDtypeStruct((columns, channels), BF16),
        scratch_of(columns, channels), 25 * 10**8, 3 * 10**6,
        far, near, row, edge, table, mix, upstream, name="back_first", limit=10,
    )


def backward_second(far, near, row, table, mix, upstream, far_out):
    _, columns, channels = upstream.shape
    return call(
        back_second_kernel, jax.ShapeDtypeStruct(upstream.shape, BF16),
        scratch_of(columns, channels), 25 * 10**8, 3 * 10**6,
        far, near, row, table, mix, upstream, far_out, name="back_second", limit=10,
    )


def pick_kernel(field_ref, out_ref, sem):
    copy = pltpu.make_async_copy(field_ref.at[pl.ds(parity(), 1)], out_ref, sem)
    copy.start()
    copy.wait()


def pick_far(field):
    _, columns, channels = field.shape
    return pl.pallas_call(
        pick_kernel,
        out_shape=jax.ShapeDtypeStruct((1, columns, channels), BF16),
        in_specs=[pl.BlockSpec(memory_space=pl.ANY)],
        out_specs=VMEM,
        scratch_shapes=[pltpu.SemaphoreType.DMA],
        compiler_params=pltpu.CompilerParams(vmem_limit_bytes=4 * 2**20),
        cost_estimate=pl.CostEstimate(flops=0, bytes_accessed=800_000, transcendentals=0),
        name="pick",
    )(field)


def near_swap(row):
    count = lax.axis_size("lat")
    return lax.ppermute(row, "lat", [(i, i ^ 1) for i in range(count)])


def far_swap(row):
    members, count = lax.axis_size("member"), lax.axis_size("lat")
    pairs = [(i, i + 1) for i in range(1, count - 1, 2)]
    pairs += [(b, a) for a, b in pairs]
    pairs = [(m * count + a, m * count + b) for m in range(members) for a, b in pairs]
    for end in (0, count - 1):
        pairs += [(m * count + end, (m + 1) % members * count + end) for m in range(members)]
    return lax.ppermute(row, ("member", "lat"), pairs)


def edges_of(rows):
    return jnp.concatenate([rows[:, -HALF:], rows[:, :HALF]], axis=1)


def core_swap(rows):
    return lax.ppermute(rows, "lon", SWAP)


def widened(row, edges):
    return jnp.concatenate([edges[:, :HALF], row, edges[:, HALF:]], axis=1)


def local_taps(psi_value, basis_index, band_width, first_row, rows):
    offsets = jnp.arange(TAPS, dtype=jnp.int32) - HALF
    inband = jnp.abs(offsets)[None, None, :] <= band_width[:, :, None]
    value = jnp.where(inband, psi_value.astype(F32), 0.0)
    both = jnp.pad(jnp.stack([value, basis_index.astype(F32)]), ((0, 0), (1, 1), (0, 0), (0, 0)))
    value, kind = lax.dynamic_slice_in_dim(both, first_row, rows + 2, 1)
    kinds = jnp.arange(KERNELS, dtype=jnp.int32).astype(F32)
    near = jnp.where(kind[:, None] == kinds[None, :, None, None], value[:, None], 0.0)
    direct = near[1 : rows + 1]
    adjoint = jnp.stack(
        [near[offset : offset + rows, :, 2 - offset, ::-1] for offset in range(3)], axis=2
    )
    even = parity() == 0
    return jnp.concatenate(
        [jnp.where(even, taps[::-1], taps) for taps in (direct, adjoint)], axis=0
    )


def halves(part, bit):
    size = part.shape[0] // 2
    keep = lax.dynamic_slice_in_dim(part, bit * size, size, 0)
    give = lax.dynamic_slice_in_dim(part, (1 - bit) * size, size, 0)
    return keep, give


def joined(own, other, bit):
    return jnp.where(
        bit == 0, jnp.concatenate([own, other], 0), jnp.concatenate([other, own], 0)
    )


def lat_swap(rows, step):
    return lax.ppermute(rows, "lat", [(i, i ^ step) for i in range(lax.axis_size("lat"))])


def on_device(activations, cotangent, mixing, psi_value, basis_index, band_width):
    channels, rows, columns = activations.shape
    total_rows = lax.axis_size("lat") * rows
    first_row = lax.axis_index("lat") * rows
    half = channels // 2
    far_row = parity()
    field = activations.transpose(1, 2, 0)
    upstream = cotangent.transpose(1, 2, 0)
    to_input = mixing.reshape(KERNELS * channels, channels)

    far_own = pick_far(field)
    far_halo = far_swap(far_own)
    later, far_own = lax.optimization_barrier((field, far_own))
    lon = core_swap(edges_of(later))
    near_own = widened(
        lax.dynamic_slice_in_dim(later, 1 - far_row, 1, 0),
        lax.dynamic_slice_in_dim(lon, 1 - far_row, 1, 0),
    )
    near_halo = near_swap(near_own)
    to_hidden, *tables = banded_tables(
        local_taps(psi_value, basis_index, band_width, first_row, rows), mixing
    )
    far_halo, to_hidden, *tables = lax.optimization_barrier((far_halo, to_hidden, *tables))
    far_edges = core_swap(edges_of(far_halo))
    far = forward_first(
        field, lon, far_halo, far_edges, tables[1], to_hidden, upstream
    )
    far_slope = far[1]
    far_slope_halo = far_swap(far_slope[None])
    block_out, near_slope, keep, give = forward_second(
        field, lon, near_halo, tables[0], to_hidden, upstream, far,
        1.0 / total_rows,
    )
    parts = [core_swap(give[at : at + 304]) for at in range(0, give.shape[0], 304)]
    *parts, far_slope_halo = lax.optimization_barrier((*parts, far_slope_halo))
    got = jnp.concatenate(parts)
    steps = [2**at for at in range((lax.axis_size("lat") - 1).bit_length())]
    low, low_give, high, high_give, far_wide, near_wide = first_split(
        steps[:2], keep, got, far_slope, near_slope
    )
    low_got, high_got = lat_swap(low_give, steps[0]), lat_swap(high_give, steps[1])
    far_slope_edges = core_swap(edges_of(far_slope_halo))
    far_grad = backward_first(
        far_wide, near_wide, far_slope_halo, far_slope_edges, tables[3], to_input, upstream
    )
    low, low_give = split(steps[1], low, low_got)
    high, high_give = split(steps[0], high, high_got)
    low_got, high_got = lat_swap(low_give, steps[1]), lat_swap(high_give, steps[0])
    high_got, near_wide = lax.optimization_barrier((high_got, near_wide))
    near_slope_halo = near_swap(near_wide)
    mine = jnp.concatenate([low, high])
    got = jnp.concatenate([low_got, high_got])
    for step in steps[2:-1]:
        mine, give = split(step, mine, got)
        got = lat_swap(give, step)
    own = added(round_kernel, mine, got)
    arrived = lat_swap(own, steps[-1])
    arrived, far_grad = lax.optimization_barrier((arrived, far_grad))
    own = added(total_kernel, own, arrived)
    for step in reversed(steps[2:-1]):
        own = join(step, own, lat_swap(own, step))
    low, high = jnp.split(own, 2)
    low_got, high_got = lat_swap(low, steps[1]), lat_swap(high, steps[0])
    low, high = join(steps[1], low, low_got), join(steps[0], high, high_got)
    low, high, near_slope_halo = lax.optimization_barrier((low, high, near_slope_halo))
    low_got, high_got = lat_swap(low, steps[0]), lat_swap(high, steps[1])
    grad_input = backward_second(
        far_wide, near_wide, near_slope_halo, tables[2], to_input, upstream, far_grad
    )
    low_got, high_got, grad_input = lax.optimization_barrier((low_got, high_got, grad_input))
    low, high = join(steps[0], low, low_got), join(steps[1], high, high_got)
    bases = (0, low.shape[0])
    low_other, high_other = core_swap(low), core_swap(high)
    grad_mixing = placed(mixing.shape, bases, (low, high), "own")
    grad_mixing, low_other = lax.optimization_barrier((grad_mixing, low_other))
    grad_mixing = placed(
        mixing.shape, bases, (low_other, high_other), "other", grad_mixing
    )
    return block_out.transpose(2, 0, 1), grad_input.transpose(2, 0, 1), grad_mixing


def solution(mesh):
    in_specs = (P("member", "lat", "lon"), P("member", "lat", "lon"), P(), P(), P(), P())
    out_specs = (P("member", "lat", "lon"), P("member", "lat", "lon"), P("member", None, None))
    return jax.shard_map(
        on_device, mesh=mesh, in_specs=in_specs, out_specs=out_specs, check_vma=False
    )
```

```python
import math

import jax
import jax.numpy as jnp
from jax import lax
from jax.experimental import pallas as pl
from jax.experimental.pallas import tpu as pltpu
from jax.sharding import PartitionSpec as P

KERNELS = 9
HALF = 16
TAPS = 2 * HALF + 1
BLK = 128
WIN = BLK + 2 * HALF
DEPTH = 512
STEP = 240
SWAP = [(0, 1), (1, 0)]
VMEM = pl.BlockSpec(memory_space=pltpu.VMEM)
BF16, F32 = jnp.bfloat16, jnp.float32


def call(kernel, out_shape, scratch, flops, size, *operands, name, limit):
    return pl.pallas_call(
        kernel,
        out_shape=out_shape,
        in_specs=[VMEM] * len(operands),
        out_specs=jax.tree.map(lambda _: VMEM, out_shape),
        scratch_shapes=scratch,
        compiler_params=pltpu.CompilerParams(vmem_limit_bytes=limit * 2**20),
        cost_estimate=pl.CostEstimate(flops=flops, bytes_accessed=size, transcendentals=0),
        name=name,
    )(*operands)


def tables_kernel(lines_ref, mixing_ref, turned_ref, *out_refs):
    channels = mixing_ref.shape[2]
    for kind in range(KERNELS):
        turned_ref[kind * channels : (kind + 1) * channels] = mixing_ref[kind].T
    for row, out_ref in enumerate(out_refs):
        for kind in range(KERNELS):
            line = jnp.broadcast_to(lines_ref[row, kind : kind + 1, :], (BLK, DEPTH))
            out_ref[kind * BLK : (kind + 1) * BLK, :] = pltpu.roll(
                line, 0, 1, stride=1, stride_axis=0
            ).astype(BF16)


def banded_tables(taps, mixing):
    lead = taps.shape[0]
    kinds, channels, _ = mixing.shape
    lines = jnp.pad(taps.astype(F32), ((0, 0), (0, 0), (0, 0), (0, WIN - TAPS)))
    lines = jnp.pad(lines.reshape(lead, KERNELS, 3 * WIN), ((0, 0), (0, 0), (0, DEPTH - 3 * WIN)))
    turned = jax.ShapeDtypeStruct((kinds * channels, channels), BF16)
    shapes = [turned] + [jax.ShapeDtypeStruct((KERNELS * BLK, DEPTH), BF16)] * lead
    return call(
        tables_kernel, shapes, [], 10**7, 3_000_000, lines, mixing, name="tables", limit=12
    )


def parity():
    return lax.rem(lax.axis_index("lat"), 2)


def place(wide_ref, slot, middle, edges):
    columns = middle.shape[0]
    wide_ref[slot, 0:HALF] = edges[0:HALF]
    wide_ref[slot, HALF : HALF + columns] = middle
    wide_ref[slot, HALF + columns :] = edges[HALF:]


def place_inside(wide_ref, slot, middle_ref, edges_ref):
    lat = lax.axis_index("lat")
    inside = (lat > 0) & (lat < lax.axis_size("lat") - 1)

    @pl.when(inside)
    def _():
        place(wide_ref, slot, middle_ref[0], edges_ref[0])

    @pl.when(jnp.logical_not(inside))
    def _():
        wide_ref[slot] = jnp.zeros(wide_ref.shape[1:], BF16)


def banded_row(table_ref, wide_ref, buffer_ref):
    columns = buffer_ref.shape[0]
    channels = wide_ref.shape[2]
    for block in range(-(-columns // BLK)):
        start = min(block * BLK, columns - BLK)
        window = jnp.concatenate(
            [wide_ref[offset, start : start + WIN] for offset in range(3)], axis=0
        )
        for kind in range(KERNELS):
            out = jnp.dot(
                table_ref[kind * BLK : (kind + 1) * BLK, : 3 * WIN],
                window,
                preferred_element_type=F32,
            )
            buffer_ref[start : start + BLK, kind * channels : (kind + 1) * channels] = (
                out.astype(BF16)
            )


def gelu_parts(hidden):
    cdf = 0.5 * (1.0 + lax.erf(hidden * (1.0 / math.sqrt(2.0))))
    slope = cdf + hidden * jnp.exp(-0.5 * hidden * hidden) * (1.0 / math.sqrt(2.0 * math.pi))
    return hidden * cdf, slope


def gelu_row(field_ref, cot_ref, row, mix_ref, buffer_ref, out_ref, slope_ref, turned_ref):
    columns = buffer_ref.shape[0]
    for start in range(0, columns, STEP):
        part = slice(start, start + STEP)
        hidden = jnp.dot(buffer_ref[part, :], mix_ref[...], preferred_element_type=F32)
        value, derivative = gelu_parts(hidden)
        out_ref[part] = (field_ref[row, part].astype(F32) + value).astype(BF16)
        slope_ref[part] = (cot_ref[row, part].astype(F32) * derivative).astype(BF16)
    turned_ref[...] = slope_ref[...].T


def grad_of(turned_ref, buffer_ref, kind):
    channels = turned_ref.shape[0]
    return jnp.dot(
        turned_ref[...],
        buffer_ref[:, kind * channels : (kind + 1) * channels],
        preferred_element_type=F32,
    )


def first_kernel(
    field_ref, lon_ref, row_ref, edge_ref, table_ref, mix_ref, cot_ref,
    out_ref, slope_ref, buffer_ref, turned_ref, wide_ref,
):
    odd = parity()
    near, far = 1 - odd, odd
    place(wide_ref, 2 - 2 * odd, field_ref[near], lon_ref[near])
    place(wide_ref, 1, field_ref[far], lon_ref[far])
    place_inside(wide_ref, 2 * odd, row_ref, edge_ref)
    banded_row(table_ref, wide_ref, buffer_ref)
    gelu_row(field_ref, cot_ref, far, mix_ref, buffer_ref, out_ref, slope_ref, turned_ref)


def second_kernel(
    scale, field_ref, lon_ref, row_ref, table_ref, mix_ref, cot_ref,
    far_out_ref, far_slope_ref, far_buffer_ref, far_turned_ref,
    out_ref, slope_ref, keep_ref, give_ref, wide_ref, buffer_ref, turned_ref,
):
    odd = parity()
    near, far = 1 - odd, odd
    place(wide_ref, 2 * odd, field_ref[far], lon_ref[far])
    place(wide_ref, 1, field_ref[near], lon_ref[near])
    wide_ref[2 - 2 * odd] = row_ref[0]
    banded_row(table_ref, wide_ref, buffer_ref)
    gelu_row(
        field_ref, cot_ref, near, mix_ref, buffer_ref, out_ref.at[near], slope_ref, turned_ref
    )
    out_ref[far] = far_out_ref[...]
    first = lax.axis_index("lon") == 0
    columns = slope_ref.shape[0]
    channels = turned_ref.shape[0]
    half = channels // 2
    for kind in range(KERNELS):
        grad = scale * (
            grad_of(far_turned_ref, far_buffer_ref, kind)
            + grad_of(turned_ref, buffer_ref, kind)
        )
        low, high = grad[:half], grad[half:]
        part = slice(kind * half, (kind + 1) * half)
        keep_ref[part] = jnp.where(first, low, high)
        give_ref[part] = jnp.where(first, high, low).astype(BF16)
    base = KERNELS * half
    for ref in (far_slope_ref, slope_ref):
        give_ref[base : base + HALF] = ref[columns - HALF :]
        give_ref[base + HALF : base + 2 * HALF] = ref[:HALF]
        base += 2 * HALF


def contract_row(cot_ref, row, mix_ref, buffer_ref, out_ref):
    columns = buffer_ref.shape[0]
    for start in range(0, columns, STEP):
        part = slice(start, start + STEP)
        grad = jnp.dot(buffer_ref[part, :], mix_ref[...], preferred_element_type=F32)
        out_ref[part] = (cot_ref[row, part].astype(F32) + grad).astype(BF16)


def back_first_kernel(
    far_ref, near_ref, row_ref, edge_ref, table_ref, mix_ref, cot_ref,
    out_ref, wide_ref, buffer_ref,
):
    odd = parity()
    wide_ref[2 - 2 * odd] = near_ref[0]
    wide_ref[1] = far_ref[0]
    place_inside(wide_ref, 2 * odd, row_ref, edge_ref)
    banded_row(table_ref, wide_ref, buffer_ref)
    contract_row(cot_ref, odd, mix_ref, buffer_ref, out_ref)


def back_second_kernel(
    far_ref, near_ref, row_ref, table_ref, mix_ref, cot_ref, far_out_ref,
    out_ref, wide_ref, buffer_ref,
):
    odd = parity()
    wide_ref[2 * odd] = far_ref[0]
    wide_ref[1] = near_ref[0]
    wide_ref[2 - 2 * odd] = row_ref[0]
    banded_row(table_ref, wide_ref, buffer_ref)
    contract_row(cot_ref, 1 - odd, mix_ref, buffer_ref, out_ref.at[1 - odd])
    out_ref[odd] = far_out_ref[...]


def lat_bit_clear(step):
    return lax.rem(lax.div(lax.axis_index("lat"), step), 2) == 0


def first_split_kernel(
    steps, keep_ref, got_ref, far_ref, near_ref,
    low_mine_ref, low_give_ref, high_mine_ref, high_give_ref, far_wide_ref, near_wide_ref,
):
    base = keep_ref.shape[0]
    half = base // 2
    split_kernel(
        steps[0], keep_ref.at[pl.ds(0, half)], got_ref.at[pl.ds(0, half)], low_mine_ref, low_give_ref
    )
    split_kernel(
        steps[1], keep_ref.at[pl.ds(half, half)], got_ref.at[pl.ds(half, half)], high_mine_ref, high_give_ref
    )
    for row_ref, wide_ref in ((far_ref, far_wide_ref), (near_ref, near_wide_ref)):
        columns = row_ref.shape[0]
        wide_ref[0, :HALF] = got_ref[base : base + HALF]
        wide_ref[0, HALF : HALF + columns] = row_ref[...]
        wide_ref[0, HALF + columns :] = got_ref[base + HALF : base + 2 * HALF]
        base += 2 * HALF


def split_kernel(step, keep_ref, got_ref, mine_ref, give_ref):
    half = keep_ref.shape[0] // 2
    clear = lat_bit_clear(step)
    low = keep_ref[:half] + got_ref[:half].astype(F32)
    high = keep_ref[half:] + got_ref[half : 2 * half].astype(F32)
    mine_ref[...] = jnp.where(clear, low, high)
    give_ref[...] = jnp.where(clear, high, low).astype(BF16)


def join_kernel(step, own_ref, got_ref, out_ref):
    half = own_ref.shape[0]
    clear = lat_bit_clear(step)
    out_ref[:half] = jnp.where(clear, own_ref[...], got_ref[...])
    out_ref[half:] = jnp.where(clear, got_ref[...], own_ref[...])


def round_kernel(keep_ref, got_ref, out_ref):
    out_ref[...] = (keep_ref[...] + got_ref[...].astype(F32)).astype(BF16)


def total_kernel(own_ref, got_ref, out_ref):
    out_ref[...] = (own_ref[...].astype(F32) + got_ref[...].astype(F32)).astype(BF16)


def place_kernel(parts, column_of, *refs):
    given = refs[: len(parts)]
    out_ref, stage_ref, sems = refs[-3:]
    half = out_ref.shape[1] // 2
    column = lax.axis_index("lon")
    if column_of == "other":
        column = 1 - column
    copies = []
    at = 0
    for base, ref in zip(parts, given):
        row, end = base, base + ref.shape[0]
        while row < end:
            count = min(half - row % half, end - row)
            stage_ref[at : at + count] = ref[row - base : row - base + count].astype(F32)
            start = pl.multiple_of(row % half + column * half, 64)
            copy = pltpu.make_async_copy(
                stage_ref.at[pl.ds(at, count)],
                out_ref.at[row // half, pl.ds(start, count)],
                sems.at[len(copies)],
            )
            copy.start()
            copies.append(copy)
            row, at = row + count, at + count
    for copy in copies:
        copy.wait()


def placed(shape, parts, given, column_of, *before):
    rows, channels = sum(part.shape[0] for part in given), shape[2]

    def kernel(*refs):
        place_kernel(parts, column_of, *refs)

    anywhere = pl.BlockSpec(memory_space=pl.ANY)
    return pl.pallas_call(
        kernel,
        out_shape=jax.ShapeDtypeStruct(shape, F32),
        in_specs=[VMEM] * len(given) + [anywhere] * len(before),
        out_specs=anywhere,
        scratch_shapes=[pltpu.VMEM((rows, channels), F32), pltpu.SemaphoreType.DMA((16,))],
        input_output_aliases={len(given): 0} if before else {},
        compiler_params=pltpu.CompilerParams(vmem_limit_bytes=8 * 2**20),
        cost_estimate=pl.CostEstimate(flops=0, bytes_accessed=10**6, transcendentals=0),
        name="placed",
    )(*given, *before)


def glue(kernel, shapes, *operands, name):
    return call(kernel, shapes, [], 10**6, 10**6, *operands, name=name, limit=8)


def tiled(rows):
    return rows % 16 == 0


def bit_of(step):
    return (lax.axis_index("lat") // step) % 2


def split(step, keep, got):
    rows, channels = keep.shape
    if not tiled(rows // 2):
        whole = keep + got.astype(F32)
        mine, give = halves(whole, bit_of(step))
        return mine, give.astype(BF16)

    def kernel(*refs):
        split_kernel(step, *refs)

    shapes = (
        jax.ShapeDtypeStruct((rows // 2, channels), F32),
        jax.ShapeDtypeStruct((rows // 2, channels), BF16),
    )
    return glue(kernel, shapes, keep, got, name="split")


def first_split(steps, keep, got, far, near):
    rows, channels = keep.shape

    def kernel(*refs):
        first_split_kernel(steps, *refs)

    wide = jax.ShapeDtypeStruct((1, far.shape[0] + 2 * HALF, channels), BF16)
    mine = jax.ShapeDtypeStruct((rows // 4, channels), F32)
    give = jax.ShapeDtypeStruct((rows // 4, channels), BF16)
    shapes = (mine, give, mine, give, wide, wide)
    return glue(kernel, shapes, keep, got, far, near, name="first_split")


def join(step, own, got):
    rows, channels = own.shape
    if not tiled(rows):
        return joined(own, got, bit_of(step))

    def kernel(*refs):
        join_kernel(step, *refs)

    return glue(
        kernel, jax.ShapeDtypeStruct((2 * rows, channels), BF16), own, got, name="join"
    )


def added(kernel, own, got):
    if not tiled(own.shape[0]):
        return (own.astype(F32) + got.astype(F32)).astype(BF16)
    return glue(kernel, jax.ShapeDtypeStruct(own.shape, BF16), own, got, name="added")


def scratch_of(columns, channels):
    return [
        pltpu.VMEM((3, columns + 2 * HALF, channels), BF16),
        pltpu.VMEM((columns, KERNELS * channels), BF16),
    ]


def forward_first(field, lon, row, edge, table, mix, upstream):
    _, columns, channels = field.shape
    shapes = (
        jax.ShapeDtypeStruct((columns, channels), BF16),
        jax.ShapeDtypeStruct((columns, channels), BF16),
        jax.ShapeDtypeStruct((columns, KERNELS * channels), BF16),
        jax.ShapeDtypeStruct((channels, columns), BF16),
    )
    return call(
        first_kernel, shapes, scratch_of(columns, channels)[:1], 25 * 10**8, 4 * 10**6,
        field, lon, row, edge, table, mix, upstream, name="first", limit=16,
    )


def forward_second(field, lon, row, table, mix, upstream, far, scale):
    _, columns, channels = field.shape
    half = KERNELS * channels // 2
    shapes = (
        jax.ShapeDtypeStruct(field.shape, BF16),
        jax.ShapeDtypeStruct((columns, channels), BF16),
        jax.ShapeDtypeStruct((half, channels), F32),
        jax.ShapeDtypeStruct((half + 4 * HALF, channels), BF16),
    )
    turned = pltpu.VMEM((channels, columns), BF16)

    def kernel(*refs):
        second_kernel(scale, *refs)

    return call(
        kernel, shapes, scratch_of(columns, channels) + [turned], 35 * 10**8, 4 * 10**6,
        field, lon, row, table, mix, upstream, *far,
        name="second", limit=16,
    )


def backward_first(far, near, row, edge, table, mix, upstream):
    _, columns, channels = upstream.shape
    return call(
        back_first_kernel, jax.ShapeDtypeStruct((columns, channels), BF16),
        scratch_of(columns, channels), 25 * 10**8, 3 * 10**6,
        far, near, row, edge, table, mix, upstream, name="back_first", limit=10,
    )


def backward_second(far, near, row, table, mix, upstream, far_out):
    _, columns, channels = upstream.shape
    return call(
        back_second_kernel, jax.ShapeDtypeStruct(upstream.shape, BF16),
        scratch_of(columns, channels), 25 * 10**8, 3 * 10**6,
        far, near, row, table, mix, upstream, far_out, name="back_second", limit=10,
    )


def near_swap(row):
    count = lax.axis_size("lat")
    return lax.ppermute(row, "lat", [(i, i ^ 1) for i in range(count)])


def far_swap(row):
    members, count = lax.axis_size("member"), lax.axis_size("lat")
    pairs = [(i, i + 1) for i in range(1, count - 1, 2)]
    pairs += [(b, a) for a, b in pairs]
    pairs = [(m * count + a, m * count + b) for m in range(members) for a, b in pairs]
    for end in (0, count - 1):
        pairs += [(m * count + end, (m + 1) % members * count + end) for m in range(members)]
    return lax.ppermute(row, ("member", "lat"), pairs)


def edges_of(rows):
    return jnp.concatenate([rows[:, -HALF:], rows[:, :HALF]], axis=1)


def core_swap(rows):
    return lax.ppermute(rows, "lon", SWAP)


def widened(row, edges):
    return jnp.concatenate([edges[:, :HALF], row, edges[:, HALF:]], axis=1)


def local_taps(psi_value, basis_index, band_width, first_row, rows):
    offsets = jnp.arange(TAPS, dtype=jnp.int32) - HALF
    inband = jnp.abs(offsets)[None, None, :] <= band_width[:, :, None]
    value = jnp.where(inband, psi_value.astype(F32), 0.0)
    both = jnp.pad(jnp.stack([value, basis_index.astype(F32)]), ((0, 0), (1, 1), (0, 0), (0, 0)))
    value, kind = lax.dynamic_slice_in_dim(both, first_row, rows + 2, 1)
    kinds = jnp.arange(KERNELS, dtype=jnp.int32).astype(F32)
    near = jnp.where(kind[:, None] == kinds[None, :, None, None], value[:, None], 0.0)
    direct = near[1 : rows + 1]
    adjoint = jnp.stack(
        [near[offset : offset + rows, :, 2 - offset, ::-1] for offset in range(3)], axis=2
    )
    even = parity() == 0
    return jnp.concatenate(
        [jnp.where(even, taps[::-1], taps) for taps in (direct, adjoint)], axis=0
    )


def halves(part, bit):
    size = part.shape[0] // 2
    keep = lax.dynamic_slice_in_dim(part, bit * size, size, 0)
    give = lax.dynamic_slice_in_dim(part, (1 - bit) * size, size, 0)
    return keep, give


def joined(own, other, bit):
    return jnp.where(
        bit == 0, jnp.concatenate([own, other], 0), jnp.concatenate([other, own], 0)
    )


def lat_swap(rows, step):
    return lax.ppermute(rows, "lat", [(i, i ^ step) for i in range(lax.axis_size("lat"))])


def on_device(activations, cotangent, mixing, psi_value, basis_index, band_width):
    channels, rows, columns = activations.shape
    total_rows = lax.axis_size("lat") * rows
    first_row = lax.axis_index("lat") * rows
    half = channels // 2
    far_row = parity()
    field = activations.transpose(1, 2, 0)
    upstream = cotangent.transpose(1, 2, 0)
    to_input = mixing.reshape(KERNELS * channels, channels)

    far_own = jnp.where(far_row == 0, field[:1], field[1:])
    far_halo = far_swap(far_own)
    later, far_own = lax.optimization_barrier((field, far_own))
    lon = core_swap(edges_of(later))
    near_own = widened(
        lax.dynamic_slice_in_dim(later, 1 - far_row, 1, 0),
        lax.dynamic_slice_in_dim(lon, 1 - far_row, 1, 0),
    )
    near_halo = near_swap(near_own)
    to_hidden, *tables = banded_tables(
        local_taps(psi_value, basis_index, band_width, first_row, rows), mixing
    )
    far_halo, to_hidden, *tables = lax.optimization_barrier((far_halo, to_hidden, *tables))
    far_edges = core_swap(edges_of(far_halo))
    far = forward_first(
        field, lon, far_halo, far_edges, tables[1], to_hidden, upstream
    )
    far_slope = far[1]
    far_slope_halo = far_swap(far_slope[None])
    block_out, near_slope, keep, give = forward_second(
        field, lon, near_halo, tables[0], to_hidden, upstream, far,
        1.0 / total_rows,
    )
    parts = [core_swap(give[at : at + 304]) for at in range(0, give.shape[0], 304)]
    *parts, far_slope_halo = lax.optimization_barrier((*parts, far_slope_halo))
    got = jnp.concatenate(parts)
    steps = [2**at for at in range((lax.axis_size("lat") - 1).bit_length())]
    low, low_give, high, high_give, far_wide, near_wide = first_split(
        steps[:2], keep, got, far_slope, near_slope
    )
    low_got, high_got = lat_swap(low_give, steps[0]), lat_swap(high_give, steps[1])
    far_slope_edges = core_swap(edges_of(far_slope_halo))
    far_grad = backward_first(
        far_wide, near_wide, far_slope_halo, far_slope_edges, tables[3], to_input, upstream
    )
    low, low_give = split(steps[1], low, low_got)
    high, high_give = split(steps[0], high, high_got)
    low_got, high_got = lat_swap(low_give, steps[1]), lat_swap(high_give, steps[0])
    high_got, near_wide = lax.optimization_barrier((high_got, near_wide))
    near_slope_halo = near_swap(near_wide)
    mine = jnp.concatenate([low, high])
    got = jnp.concatenate([low_got, high_got])
    for step in steps[2:-1]:
        mine, give = split(step, mine, got)
        got = lat_swap(give, step)
    own = added(round_kernel, mine, got)
    arrived = lat_swap(own, steps[-1])
    arrived, far_grad = lax.optimization_barrier((arrived, far_grad))
    own = added(total_kernel, own, arrived)
    for step in reversed(steps[2:-1]):
        own = join(step, own, lat_swap(own, step))
    low, high = jnp.split(own, 2)
    low_got, high_got = lat_swap(low, steps[1]), lat_swap(high, steps[0])
    low, high = join(steps[1], low, low_got), join(steps[0], high, high_got)
    low, high, near_slope_halo = lax.optimization_barrier((low, high, near_slope_halo))
    low_got, high_got = lat_swap(low, steps[0]), lat_swap(high, steps[1])
    grad_input = backward_second(
        far_wide, near_wide, near_slope_halo, tables[2], to_input, upstream, far_grad
    )
    low_got, high_got, grad_input = lax.optimization_barrier((low_got, high_got, grad_input))
    low, high = join(steps[0], low, low_got), join(steps[1], high, high_got)
    bases = (0, low.shape[0])
    low_other, high_other = core_swap(low), core_swap(high)
    grad_mixing = placed(mixing.shape, bases, (low, high), "own")
    grad_mixing, low_other = lax.optimization_barrier((grad_mixing, low_other))
    grad_mixing = placed(
        mixing.shape, bases, (low_other, high_other), "other", grad_mixing
    )
    return block_out.transpose(2, 0, 1), grad_input.transpose(2, 0, 1), grad_mixing


def solution(mesh):
    in_specs = (P("member", "lat", "lon"), P("member", "lat", "lon"), P(), P(), P(), P())
    out_specs = (P("member", "lat", "lon"), P("member", "lat", "lon"), P("member", None, None))
    return jax.shard_map(
        on_device, mesh=mesh, in_specs=in_specs, out_specs=out_specs, check_vma=False
    )
```
